256 devices in a mesh: ctx: 64 (over x, y, z_hi, core), ch: 4 (over z_lo).
Axes of the slice: x: 4, y: 4, z: 8 (z_hi: 2, z_lo: 4; z = z_hi * 4 + z_lo), core: 2. Of those that a mesh axis runs over, the one named last changes fastest.
Arguments:
- out_gate: bfloat16 [16384, 4096], P('ctx', 'ch'), may hold values from -6 to 6
- in_gate: bfloat16 [16384, 4096], P('ctx', 'ch'), may hold values from -6 to 6
- values: bfloat16 [16384, 4096], P('ctx', 'ch'), may hold values from -6 to 6
- filter_taps: bfloat16 [16384, 4096], P('ctx', 'ch'), may hold values from -0.046875 to 0.046875
- out_grad: bfloat16 [16384, 4096], P('ctx'), may hold values from -16 to 16
- out_weight: bfloat16 [4096, 4096], P('ch', 'ctx'), may hold values from -0.09375 to 0.09375
Outputs:
- out_gate_grad: bfloat16 [16384, 4096], P('ctx', 'ch')
- in_gate_grad: bfloat16 [16384, 4096], P('ctx', 'ch')
- values_grad: bfloat16 [16384, 4096], P('ctx', 'ch')
- taps_grad: float32 [16384, 4096], P('ctx', 'ch')
- weight_grad: float32 [4096, 4096], P('ch', 'ctx')
The draws below stay inside these ranges and needn't reach their ends.
All inputs are finite; a program needn't handle non-finite values.
Results may differ from the reference program's by a relative error of at most 0.0065.
Values may be sent and summed in bfloat16 or wider, within the bound.
A program may use at most 128 MiB of HBM per device.

```python
import jax
import jax.numpy as jnp
from jax import lax

D = 4096
SEQ = 16384


def raised(drawn, own_key, source, target, blocks, factor):
    owner, partner = [(jnp.arange(drawn.shape[position]) // (drawn.shape[position] // blocks)).reshape([-1 if axis == position else 1 for axis in range(drawn.ndim)]) for position in (source, target)]
    chosen = jax.random.permutation(own_key, blocks)[partner]
    strong = (owner == chosen) | (owner == (partner + blocks // 2) % blocks)
    return jnp.where(strong, factor * drawn, drawn)


def steps_of(stream_key, shape, shards, low, high):
    factor_of = 1.0
    for dim, blocks in shards:
        draws = jax.random.uniform(jax.random.fold_in(jax.random.fold_in(stream_key, 6), dim), (blocks,), jnp.float32, low / len(shards), high / len(shards))
        factor_of = factor_of * jnp.repeat(jnp.exp(draws), shape[dim] // blocks).reshape((-1,) + (1,) * (len(shape) - 1 - dim))
    return factor_of


def scatter_about(own_key, shape, spread, reach, pieces=(), kind=jnp.bfloat16):
    result = spread * jax.random.normal(own_key, shape, jnp.float32)
    if pieces:
        result = result * steps_of(own_key, shape, pieces, -0.22, 0.18)
    return jnp.clip(result, -reach, reach).astype(kind)


def gaussian_with(rng, shape, scale, limit, split, heavy, held_as=jnp.bfloat16):
    values = scale * jax.random.normal(rng, shape, jnp.float32)
    if split:
        values = values * steps_of(rng, shape, split, -0.22, 0.18)
    return jnp.clip(raised(values, jax.random.fold_in(rng, 3), *heavy), -limit, limit).astype(held_as)


def setup_inputs(seed: int = 0) -> dict:
    keys = jax.random.split(jax.random.key(seed), 7)
    out_gate = scatter_about(keys[0], (SEQ, D), 1.0, 6.0, ((0, 64), (1, 4)))
    in_gate = scatter_about(keys[1], (SEQ, D), 1.0, 6.0, ((0, 64), (1, 4)))
    values = scatter_about(keys[2], (SEQ, D), 1.0, 6.0, ((0, 64), (1, 4)))
    filter_taps = scatter_about(keys[3], (SEQ, D), SEQ ** -0.5, 0.046875, ((0, 64), (1, 4)))
    out_grad = gaussian_with(keys[4], (SEQ, D), 1.0, 16.0, ((0, 64),), (0, 1, 64, 4.0))
    out_weight = scatter_about(keys[5], (D, D), D ** -0.5, 0.09375, ((0, 4), (1, 64)))
    return {"out_gate": out_gate, "in_gate": in_gate, "values": values, "filter_taps": filter_taps, "out_grad": out_grad, "out_weight": out_weight}


def spectral_block(block):
    gated_blk, grad_blk, taps_blk = block
    length = gated_blk.shape[1]
    size = 2 * length
    spec_gated = jnp.fft.rfft(gated_blk, n=size, axis=1)
    spec_grad = jnp.fft.rfft(grad_blk, n=size, axis=1)
    spec_taps = jnp.fft.rfft(taps_blk, n=size, axis=1)
    conv = jnp.fft.irfft(spec_taps * spec_gated, n=size, axis=1)[:, :length]
    grad_gated = jnp.fft.irfft(jnp.conj(spec_taps) * spec_grad, n=size, axis=1)[:, :length]
    taps_grad = jnp.fft.irfft(jnp.conj(spec_gated) * spec_grad, n=size, axis=1)[:, :length]
    return conv.astype(jnp.float32), grad_gated.astype(jnp.float32), taps_grad.astype(jnp.float32)


def reference(out_gate, in_gate, values, filter_taps, out_grad, out_weight):
    length, width = out_gate.shape
    grad_y = jnp.dot(out_grad, out_weight.T, preferred_element_type=jnp.float32).astype(jnp.bfloat16)
    gated = (in_gate.astype(jnp.float32) * values.astype(jnp.float32)).astype(jnp.bfloat16)
    grad_conv = (grad_y.astype(jnp.float32) * out_gate.astype(jnp.float32)).astype(jnp.bfloat16)
    block_width = min(64, width)
    blocks = width // block_width

    def channel_major(array):
        return array.astype(jnp.float32).T.reshape(blocks, block_width, length)

    conv_all, grad_all, taps_all = lax.map(spectral_block, (channel_major(gated), channel_major(grad_conv), channel_major(filter_taps)))
    conv = conv_all.reshape(width, length).T.astype(jnp.bfloat16)
    grad_gated = grad_all.reshape(width, length).T.astype(jnp.bfloat16)
    taps_grad = taps_all.reshape(width, length).T
    out_gate_grad = (grad_y.astype(jnp.float32) * conv.astype(jnp.float32)).astype(jnp.bfloat16)
    in_gate_grad = (grad_gated.astype(jnp.float32) * values.astype(jnp.float32)).astype(jnp.bfloat16)
    values_grad = (grad_gated.astype(jnp.float32) * in_gate.astype(jnp.float32)).astype(jnp.bfloat16)
    mixed = (out_gate.astype(jnp.float32) * conv.astype(jnp.float32)).astype(jnp.bfloat16)
    weight_grad = jnp.dot(mixed.T, out_grad, preferred_element_type=jnp.float32)
    return out_gate_grad, in_gate_grad, values_grad, taps_grad, weight_grad
```

```python
import functools

import jax
import jax.numpy as jnp
import numpy as np
from jax import lax
from jax.experimental import pallas as pl
from jax.experimental.pallas import tpu as pltpu
from jax.sharding import PartitionSpec as P

MESH = pl.DeviceIdType.MESH
F32 = jnp.float32
BF16 = jnp.bfloat16

RANKS = 64
POS = 256
CHAN = 16
WIDTH = RANKS * CHAN
MODEL = 4096
VMEM_LIMIT = 56 * 2**20


def coords():
    i = lax.axis_index("ctx")
    return i // 16, (i // 4) % 4, (i // 2) % 2, i % 2


def device(x, y, z, b):
    return (((x * 4 + y) * 2 + z) * 2 + b, lax.axis_index("ch"))


def split(x):
    hi = x.astype(BF16)
    return hi, (x - hi.astype(F32)).astype(BF16)


def tables():
    n = RANKS * POS
    k1 = np.arange(RANKS) + 0.25
    first = 2 * np.pi * k1[:, None] * np.arange(RANKS)[None, :] / RANKS
    turn = 2 * np.pi * k1[:, None] * np.arange(POS)[None, :] / n
    second = 2 * np.pi * ((np.arange(POS)[:, None] * np.arange(POS)[None, :]) % POS) / POS

    def parts(table):
        hi = table.astype(jnp.bfloat16)
        lo = (table - hi.astype(np.float64)).astype(jnp.bfloat16)
        return hi, lo

    one = np.concatenate([np.cos(first), -np.sin(first)], 0)
    one_hi, one_lo = parts(one)
    cos, sin = np.cos(second), np.sin(second)
    two_hi, two_lo = parts(np.block([[cos, -sin], [sin, cos]]))
    last = np.concatenate([np.cos(first), np.sin(first)], 0).T / n
    last_hi, last_lo = parts(last)
    return (
        np.concatenate([one_hi, one_lo], 1),
        np.cos(turn).astype(np.float32),
        (-np.sin(turn)).astype(np.float32),
        two_hi,
        two_lo,
        np.concatenate([last_hi, last_lo, last_hi], 1),
    )


def transform(rows, tabs, z_hi, z_lo, spec):
    one, cos_t, sin_t, two_hi, two_lo, _ = tabs
    for c in range(CHAN):
        x = jnp.concatenate([rows[u, pl.ds(c, RANKS, stride=CHAN), :] for u in range(2)], 1).astype(BF16)
        a = jnp.dot(one[...], jnp.concatenate([x, x], 0), preferred_element_type=F32)
        turn_in(a[:RANKS], a[RANKS:], cos_t, sin_t, z_hi, z_lo, c)
    second(z_hi, z_lo, two_hi, two_lo, spec)


def turn_in(re, im, cos_t, sin_t, z_hi, z_lo, c):
    at = slice(c * RANKS, (c + 1) * RANKS)
    z_hi[at, :POS], z_lo[at, :POS] = split(re * cos_t[...] - im * sin_t[...])
    z_hi[at, POS:], z_lo[at, POS:] = split(re * sin_t[...] + im * cos_t[...])


def second(z_hi, z_lo, two_hi, two_lo, spec):
    def block(i, carry):
        at = pl.ds(pl.multiple_of(i * 256, 256), 256)
        spec[at, :] = (
            jnp.dot(z_hi[at, :], two_hi[...], preferred_element_type=F32)
            + jnp.dot(z_hi[at, :], two_lo[...], preferred_element_type=F32)
            + jnp.dot(z_lo[at, :], two_hi[...], preferred_element_type=F32)
        )
        return carry

    lax.fori_loop(0, WIDTH // 256, block, 0)


def signal_of(tabs, z_hi, z_lo, spec, rows):
    _, cos_t, sin_t, two_hi, two_lo, last = tabs
    second(z_hi, z_lo, two_hi, two_lo, spec)
    for c in range(CHAN):
        at = slice(c * RANKS, (c + 1) * RANKS)
        re, im = spec[at, :POS], spec[at, POS:]
        hi_re, lo_re = split(re * cos_t[...] - im * sin_t[...])
        hi_im, lo_im = split(re * sin_t[...] + im * cos_t[...])
        stack = jnp.concatenate([hi_re, hi_im, hi_re, hi_im, lo_re, lo_im], 0)
        y = jnp.dot(last[...], stack, preferred_element_type=F32)
        for u in range(2):
            rows[u, pl.ds(c, RANKS, stride=CHAN), :] = y[:, u * 128 : (u + 1) * 128]


def spectral_product(left, right, conj_right, z_hi, z_lo):
    def block(i, carry):
        at = pl.ds(pl.multiple_of(i * 64, 64), 64)
        a, b, c, d = left[at, :POS], left[at, POS:], right[at, :POS], right[at, POS:]
        if conj_right:
            re, im = a * c + b * d, b * c - a * d
        else:
            re, im = a * c - b * d, -(a * d + b * c)
        z_hi[at, :POS], z_lo[at, :POS] = split(re)
        z_hi[at, POS:], z_lo[at, POS:] = split(im)
        return carry

    lax.fori_loop(0, WIDTH // 64, block, 0)


def load_rows(blocks, which, rows):
    for s in range(RANKS):
        for u in range(2):
            rows[u, s * CHAN : (s + 1) * CHAN, :] = blocks[s, which, :, u * 128 : (u + 1) * 128].astype(F32)


def store_rows(rows, blocks, which):
    for s in range(RANKS):
        for u in range(2):
            blocks[s, which, :, u * 128 : (u + 1) * 128] = rows[u, s * CHAN : (s + 1) * CHAN, :].astype(BF16)


def first_transforms(got, one, cos_t, sin_t, two_hi, two_lo, last, spec_g, spec_h, conv, rows, z_hi, z_lo, spec):
    tabs = (one, cos_t, sin_t, two_hi, two_lo, last)
    load_rows(got, 0, rows)
    transform(rows, tabs, z_hi, z_lo, spec_g)
    load_rows(got, 1, rows)
    transform(rows, tabs, z_hi, z_lo, spec_h)
    spectral_product(spec_g, spec_h, False, z_hi, z_lo)
    signal_of(tabs, z_hi, z_lo, spec, rows)
    store_rows(rows, conv, 0)


def second_transforms(got, spec_g, spec_h, one, cos_t, sin_t, two_hi, two_lo, last, out, rows, z_hi, z_lo, spec, spec_d):
    tabs = (one, cos_t, sin_t, two_hi, two_lo, last)
    load_rows(got, 1, rows)
    transform(rows, tabs, z_hi, z_lo, spec_d)
    spectral_product(spec_h, spec_d, True, z_hi, z_lo)
    signal_of(tabs, z_hi, z_lo, spec, rows)
    store_rows(rows, out, 0)
    spectral_product(spec_g, spec_d, True, z_hi, z_lo)
    signal_of(tabs, z_hi, z_lo, spec, rows)
    store_rows(rows, out, 1)


def greet():
    x, y, z, b = coords()
    barrier = pltpu.get_barrier_semaphore()

    def say(e, carry):
        pl.semaphore_signal(barrier, inc=1, device_id=partner(e), device_id_type=MESH)
        return carry

    lax.fori_loop(1, RANKS, say, 0)
    pl.semaphore_wait(barrier, RANKS - 1)


def partner(e):
    x, y, z, b = coords()
    return device((x + e // 16) % 4, (y + (e // 4) % 4) % 4, (z + (e // 2) % 2) % 2, (b + e % 2) % 2)


def block_copy(e, src, got, send_sem, recv_sem):
    there = partner(e)
    return pltpu.make_async_remote_copy(
        src_ref=src.at[there[0]],
        dst_ref=got.at[lax.axis_index("ctx")],
        send_sem=send_sem.at[e],
        recv_sem=recv_sem.at[e],
        device_id=there,
        device_id_type=MESH,
    )


def start_exchange(src, got, send_sem, recv_sem):
    def far(i, carry):
        block_copy((i // 2) * 4 + i % 2 + 2, src, got, send_sem, recv_sem).start()
        return carry

    def near(i, carry):
        block_copy((i // 2) * 4 + i % 2, src, got, send_sem, recv_sem).start()
        return carry

    lax.fori_loop(0, 32, far, 0)
    lax.fori_loop(1, 32, near, 0)
    me = lax.axis_index("ctx")
    got[me] = src[me]


def finish_exchange(src, got, send_sem, recv_sem):
    def end(e, carry):
        block_copy(e, src, got, send_sem, recv_sem).wait()
        return carry

    lax.fori_loop(1, RANKS, end, 0)


def remote(src, dst, there, send_sem, recv_sem):
    return pltpu.make_async_remote_copy(
        src_ref=src, dst_ref=dst, send_sem=send_sem, recv_sem=recv_sem, device_id=there, device_id_type=MESH
    )


def open_kernel(
    in_gate, values, taps, out_gate, shard, out_grad,
    got, grad_y, grad_conv, pair_grad,
    src, weights, turned, send_sem, recv_sem, ag_send, ag_recv, sib_send, sib_recv,
):
    x, y, z, b = coords()
    sibling = device(x, y, z, 1 - b)
    greet()
    weights[x, y, z, b] = shard[...]
    halves = (pl.ds(0, WIDTH // 2), pl.ds(WIDTH // 2, WIDTH // 2))

    def gather(slot, n, there):
        return remote(slot, slot, there, ag_send.at[n], ag_recv.at[n])

    def relay(slot, n):
        return remote(slot, slot, sibling, sib_send.at[n], sib_recv.at[n])

    far = gather(weights.at[x, y, z, b], 0, device(x, y, 1 - z, b))
    far.start()

    for n in range(WIDTH // 128):
        at = slice(n * 128, (n + 1) * 128)
        gated = (in_gate[:, at].astype(F32) * values[:, at].astype(F32)).astype(BF16).astype(F32)
        src[n * 8 : (n + 1) * 8, 0] = gated.T.astype(BF16).reshape(8, CHAN, POS)
        src[n * 8 : (n + 1) * 8, 1] = taps[:, at].astype(F32).T.astype(BF16).reshape(8, CHAN, POS)
    start_exchange(src, got, send_sem, recv_sem)

    relays = [relay(weights.at[x, y, z, b], 0)]
    relays[0].start()
    far.wait()
    stage = []
    for d in range(1, 4):
        stage.append(gather(weights.at[x, y, :, b, :, halves[0]], d, device((x + d) % 4, y, z, b)))
        stage.append(gather(weights.at[x, y, :, b, :, halves[1]], 3 + d, device(x, (y + d) % 4, z, b)))
    for copy in stage:
        copy.start()
    relays.append(relay(weights.at[x, y, 1 - z, b], 1))
    relays[1].start()

    for n in range(MODEL // 128):
        at = slice(n * 128, (n + 1) * 128)
        turned[at, :] = out_grad[:, at].astype(F32).T.astype(BF16)

    def mine(n, carry):
        at = pl.ds(pl.multiple_of(n * 128 + b * 64, 64), 64)
        pair_grad[b, pl.ds(pl.multiple_of(n * 64, 64), 64), :] = turned[at, :]
        return carry

    def theirs(n, carry):
        at = pl.ds(pl.multiple_of(n * 128 + (1 - b) * 64, 64), 64)
        kept = pl.ds(pl.multiple_of(n * 64, 64), 64)
        turned[kept, :] = turned[at, :]
        return carry

    lax.fori_loop(0, MODEL // 128, mine, 0)
    lax.fori_loop(0, MODEL // 128, theirs, 0)
    pair = remote(turned.at[pl.ds(0, MODEL // 2)], pair_grad.at[b], sibling, sib_send.at[14], sib_recv.at[14])
    pair.start()

    for copy in stage:
        copy.wait()
    stage = []
    for d in range(1, 4):
        stage.append(gather(weights.at[:, y, :, b, :, halves[0]], 6 + d, device(x, (y + d) % 4, z, b)))
        stage.append(gather(weights.at[x, :, :, b, :, halves[1]], 9 + d, device((x + d) % 4, y, z, b)))
    for copy in stage:
        copy.start()
    for d in range(1, 4):
        relays.append(relay(weights.at[(x + 4 - d) % 4, y, :, b, :, halves[0]], 1 + d))
        relays.append(relay(weights.at[x, (y + 4 - d) % 4, :, b, :, halves[1]], 4 + d))
    for copy in relays[2:]:
        copy.start()
    last = []
    for d in range(1, 4):
        stage[2 * d - 2].wait()
        last.append(relay(weights.at[:, (y + 4 - d) % 4, :, b, :, halves[0]], 7 + d))
        last[-1].start()
        stage[2 * d - 1].wait()
        last.append(relay(weights.at[(x + 4 - d) % 4, :, :, b, :, halves[1]], 10 + d))
        last[-1].start()
    for copy in relays + last:
        copy.wait()

    for n in range(WIDTH // 256):
        at = slice(n * 256, (n + 1) * 256)
        right = weights[:, :, :, :, :, at].reshape(MODEL, 256)
        product = jnp.dot(out_grad[...], right, preferred_element_type=F32).astype(BF16)
        grad_y[:, at] = product
        turned_gate = (product.astype(F32) * out_gate[:, at].astype(F32)).astype(BF16).astype(F32)
        grad_conv[n * 16 : (n + 1) * 16] = turned_gate.T.astype(BF16).reshape(16, CHAN, POS)
    pair.wait()
    finish_exchange(src, got, send_sem, recv_sem)


def middle_kernel(conv, grad_conv, got, src, send_sem, recv_sem):
    greet()
    for s in range(RANKS):
        src[s, 0] = conv[s, 0]
        src[s, 1] = grad_conv[s]
    start_exchange(src, got, send_sem, recv_sem)
    finish_exchange(src, got, send_sem, recv_sem)


def close_kernel(
    src, mixed, pair_grad,
    got, weight_grad,
    pair_mixed, send_one, recv_one, send_two, recv_two, send_three, recv_three, own,
    send_sem, recv_sem, rs_send, rs_recv,
):
    x, y, z, b = coords()
    sibling = device(x, y, z, 1 - b)
    greet()
    pair = remote(mixed, pair_mixed.at[b], sibling, rs_send.at[0], rs_recv.at[0])
    pair.start()
    start_exchange(src, got, send_sem, recv_sem)
    pair_mixed[b] = mixed[...]
    pair.wait()
    half = WIDTH // 2

    def partial(first_row, count, at):
        rows = pl.ds(pl.multiple_of(first_row, 128), count)
        return jnp.dot(pair_grad[0, rows, :], pair_mixed[0, :, at], preferred_element_type=F32) + jnp.dot(
            pair_grad[1, rows, :], pair_mixed[1, :, at], preferred_element_type=F32
        )

    lanes = (slice(0, half), slice(half, WIDTH))
    stage = []
    for d in (2, 1, 3):
        to = (x + d) % 4
        send_one[0, d - 1] = partial(to * 512, 512, lanes[0]).astype(BF16)
        copy = remote(send_one.at[0, d - 1], recv_one.at[0, d - 1], device(to, y, z, b), rs_send.at[d], rs_recv.at[d])
        copy.start()
        stage.append(copy)
        to = (y + d) % 4
        for u in range(4):
            send_one[1, d - 1, u * 128 : (u + 1) * 128, :] = partial(u * 512 + to * 128, 128, lanes[1]).astype(BF16)
        copy = remote(
            send_one.at[1, d - 1], recv_one.at[1, d - 1], device(x, to, z, b), rs_send.at[3 + d], rs_recv.at[3 + d]
        )
        copy.start()
        stage.append(copy)
    own[0] = partial(x * 512, 512, lanes[0])
    for u in range(4):
        own[1, u * 128 : (u + 1) * 128, :] = partial(u * 512 + y * 128, 128, lanes[1])
    for copy in stage:
        copy.wait()

    def summed(h, place):
        at = pl.ds(pl.multiple_of(place * 128, 128), 128)
        total = own[h, at, :]
        for d in range(3):
            total = total + recv_one[h, d, at, :].astype(F32)
        return total

    stage = []
    for d in (2, 1, 3):
        to = (y + d) % 4
        send_two[0, d - 1] = summed(0, to).astype(BF16)
        copy = remote(
            send_two.at[0, d - 1], recv_two.at[0, d - 1], device(x, to, z, b), rs_send.at[6 + d], rs_recv.at[6 + d]
        )
        copy.start()
        stage.append(copy)
        to = (x + d) % 4
        send_two[1, d - 1] = summed(1, to).astype(BF16)
        copy = remote(
            send_two.at[1, d - 1], recv_two.at[1, d - 1], device(to, y, z, b), rs_send.at[9 + d], rs_recv.at[9 + d]
        )
        copy.start()
        stage.append(copy)
    own[0, 0:128, :] = summed(0, y)
    own[1, 0:128, :] = summed(1, x)
    for copy in stage:
        copy.wait()
    for h in range(2):
        total = own[h, 0:128, :]
        for d in range(3):
            total = total + recv_two[h, d].astype(F32)
        own[h, 0:128, :] = total
    there = pl.ds(pl.multiple_of((1 - z) * 64, 64), 64)
    here = pl.ds(pl.multiple_of(z * 64, 64), 64)
    send_three[0] = own[0, there, :].astype(BF16)
    send_three[1] = own[1, there, :].astype(BF16)
    copy = remote(send_three, recv_three, device(x, y, 1 - z, b), rs_send.at[13], rs_recv.at[13])
    copy.start()
    copy.wait()
    for h in range(2):
        weight_grad[:, lanes[h]] = own[h, here, :] + recv_three[h].astype(F32)
    finish_exchange(src, got, send_sem, recv_sem)


BLOCKS = jax.ShapeDtypeStruct((RANKS, 2, CHAN, POS), BF16)
WHOLE = pl.BlockSpec(memory_space=pltpu.VMEM)
DMA = pltpu.SemaphoreType.DMA


def call(body, name, operands, outs, scratch, collective_id=None):
    if collective_id is None:
        params = pltpu.CompilerParams(vmem_limit_bytes=VMEM_LIMIT)
    else:
        params = pltpu.CompilerParams(
            collective_id=collective_id, has_side_effects=True, vmem_limit_bytes=VMEM_LIMIT
        )
    return pl.pallas_call(
        body,
        name=name,
        out_shape=outs,
        in_specs=[WHOLE] * len(operands),
        out_specs=[WHOLE] * len(outs),
        scratch_shapes=scratch,
        compiler_params=params,
    )(*operands)


def product(left, right):
    return (left.astype(F32) * right.astype(F32)).astype(BF16)


def on_device(out_gate, in_gate, values, filter_taps, out_grad, out_weight):
    tabs = [jnp.asarray(table) for table in tables()]
    shape = jax.ShapeDtypeStruct
    sems = [DMA((RANKS,)), DMA((RANKS,))]
    got_one, grad_y, grad_conv, pair_grad = call(
        open_kernel,
        "open_kernel",
        (in_gate, values, filter_taps, out_gate, out_weight.T, out_grad),
        [BLOCKS, shape((POS, WIDTH), BF16), shape((RANKS, CHAN, POS), BF16), shape((2, MODEL // 2, POS), BF16)],
        [
            pltpu.VMEM(BLOCKS.shape, BF16),
            pltpu.VMEM((4, 4, 2, 2, 64, WIDTH), BF16),
            pltpu.VMEM((MODEL, POS), BF16),
        ]
        + sems
        + [DMA((13,)), DMA((13,)), DMA((15,)), DMA((15,))],
        0,
    )
    spectrum = shape((WIDTH, 2 * POS), F32)
    work = [
        pltpu.VMEM((2, WIDTH, 128), F32),
        pltpu.VMEM((WIDTH, 2 * POS), BF16),
        pltpu.VMEM((WIDTH, 2 * POS), BF16),
        pltpu.VMEM((WIDTH, 2 * POS), F32),
    ]
    spec_g, spec_h, conv_blocks = call(
        first_transforms,
        "first_transforms",
        (got_one, *tabs),
        [spectrum, spectrum, shape((RANKS, 1, CHAN, POS), BF16)],
        work,
    )
    (got_two,) = call(
        middle_kernel, "middle_kernel", (conv_blocks, grad_conv), [BLOCKS], [pltpu.VMEM(BLOCKS.shape, BF16)] + sems, 1
    )
    (src_three,) = call(
        second_transforms,
        "second_transforms",
        (got_two, spec_g, spec_h, *tabs),
        [BLOCKS],
        work + [pltpu.VMEM((WIDTH, 2 * POS), F32)],
    )
    conv = got_two[:, 0].reshape(WIDTH, POS).T
    half = WIDTH // 2
    got_three, weight_grad = call(
        close_kernel,
        "close_kernel",
        (src_three, product(out_gate, conv), pair_grad),
        [BLOCKS, shape((64, WIDTH), F32)],
        [
            pltpu.VMEM((2, POS, WIDTH), BF16),
            pltpu.VMEM((2, 3, 512, half), BF16),
            pltpu.VMEM((2, 3, 512, half), BF16),
            pltpu.VMEM((2, 3, 128, half), BF16),
            pltpu.VMEM((2, 3, 128, half), BF16),
            pltpu.VMEM((2, 64, half), BF16),
            pltpu.VMEM((2, 64, half), BF16),
            pltpu.VMEM((2, 512, half), F32),
        ]
        + sems
        + [DMA((14,)), DMA((14,))],
        2,
    )
    grad_gated = got_three[:, 0].reshape(WIDTH, POS).T
    taps_grad = got_three[:, 1].reshape(WIDTH, POS).T.astype(F32)
    return (
        product(grad_y, conv),
        product(grad_gated, values),
        product(grad_gated, in_gate),
        taps_grad,
        weight_grad.T,
    )


def solution(mesh):
    return jax.shard_map(
        on_device,
        mesh=mesh,
        in_specs=(
            P("ctx", "ch"),
            P("ctx", "ch"),
            P("ctx", "ch"),
            P("ctx", "ch"),
            P("ctx", None),
            P("ch", "ctx"),
        ),
        out_specs=(P("ctx", "ch"), P("ctx", "ch"), P("ctx", "ch"), P("ctx", "ch"), P("ch", "ctx")),
        check_vma=False,
    )
```

```python
import functools

import jax
import jax.numpy as jnp
import numpy as np
from jax import lax
from jax.experimental import pallas as pl
from jax.experimental.pallas import tpu as pltpu
from jax.sharding import PartitionSpec as P

MESH = pl.DeviceIdType.MESH
F32 = jnp.float32
BF16 = jnp.bfloat16

RANKS = 64
POS = 256
CHAN = 16
WIDTH = RANKS * CHAN
MODEL = 4096
VMEM_LIMIT = 60 * 2**20


def coords():
    i = lax.axis_index("ctx")
    return i // 16, (i // 4) % 4, (i // 2) % 2, i % 2


def device(x, y, z, b):
    return (((x * 4 + y) * 2 + z) * 2 + b, lax.axis_index("ch"))


def split(x):
    hi = x.astype(BF16)
    return hi, (x - hi.astype(F32)).astype(BF16)


def tables():
    n = RANKS * POS
    k1 = np.arange(RANKS) + 0.25
    first = 2 * np.pi * k1[:, None] * np.arange(RANKS)[None, :] / RANKS
    turn = 2 * np.pi * k1[:, None] * np.arange(POS)[None, :] / n
    second = 2 * np.pi * ((np.arange(POS)[:, None] * np.arange(POS)[None, :]) % POS) / POS

    def parts(table):
        hi = table.astype(jnp.bfloat16)
        lo = (table - hi.astype(np.float64)).astype(jnp.bfloat16)
        return hi, lo

    one = np.concatenate([np.cos(first), -np.sin(first)], 0)
    one_hi, one_lo = parts(one)
    cos, sin = np.cos(second), np.sin(second)
    two_hi, two_lo = parts(np.block([[cos, -sin], [sin, cos]]))
    last = np.concatenate([np.cos(first), np.sin(first)], 0).T / n
    last_hi, last_lo = parts(last)
    return (
        np.concatenate([one_hi, one_lo], 1),
        np.cos(turn).astype(np.float32),
        (-np.sin(turn)).astype(np.float32),
        two_hi,
        two_lo,
        np.concatenate([last_hi, last_lo, last_hi], 1),
    )


def transform(rows, tabs, z_hi, z_lo, spec):
    one, cos_t, sin_t, two_hi, two_lo, _ = tabs
    for c in range(CHAN):
        x = jnp.concatenate([rows[u, pl.ds(c, RANKS, stride=CHAN), :] for u in range(2)], 1).astype(BF16)
        a = jnp.dot(one[...], jnp.concatenate([x, x], 0), preferred_element_type=F32)
        turn_in(a[:RANKS], a[RANKS:], cos_t, sin_t, z_hi, z_lo, c)
    second(z_hi, z_lo, two_hi, two_lo, spec)


def turn_in(re, im, cos_t, sin_t, z_hi, z_lo, c):
    at = slice(c * RANKS, (c + 1) * RANKS)
    z_hi[at, :POS], z_lo[at, :POS] = split(re * cos_t[...] - im * sin_t[...])
    z_hi[at, POS:], z_lo[at, POS:] = split(re * sin_t[...] + im * cos_t[...])


def second(z_hi, z_lo, two_hi, two_lo, spec):
    def block(i, carry):
        at = pl.ds(pl.multiple_of(i * 256, 256), 256)
        spec[at, :] = (
            jnp.dot(z_hi[at, :], two_hi[...], preferred_element_type=F32)
            + jnp.dot(z_hi[at, :], two_lo[...], preferred_element_type=F32)
            + jnp.dot(z_lo[at, :], two_hi[...], preferred_element_type=F32)
        )
        return carry

    lax.fori_loop(0, WIDTH // 256, block, 0)


def signal_of(tabs, z_hi, z_lo, spec, rows):
    _, cos_t, sin_t, two_hi, two_lo, last = tabs
    second(z_hi, z_lo, two_hi, two_lo, spec)
    for c in range(CHAN):
        at = slice(c * RANKS, (c + 1) * RANKS)
        re, im = spec[at, :POS], spec[at, POS:]
        hi_re, lo_re = split(re * cos_t[...] - im * sin_t[...])
        hi_im, lo_im = split(re * sin_t[...] + im * cos_t[...])
        stack = jnp.concatenate([hi_re, hi_im, hi_re, hi_im, lo_re, lo_im], 0)
        y = jnp.dot(last[...], stack, preferred_element_type=F32)
        for u in range(2):
            rows[u, pl.ds(c, RANKS, stride=CHAN), :] = y[:, u * 128 : (u + 1) * 128]


def spectral_product(left, right, conj_right, z_hi, z_lo):
    def block(i, carry):
        at = pl.ds(pl.multiple_of(i * 64, 64), 64)
        a, b, c, d = left[at, :POS], left[at, POS:], right[at, :POS], right[at, POS:]
        if conj_right:
            re, im = a * c + b * d, b * c - a * d
        else:
            re, im = a * c - b * d, -(a * d + b * c)
        z_hi[at, :POS], z_lo[at, :POS] = split(re)
        z_hi[at, POS:], z_lo[at, POS:] = split(im)
        return carry

    lax.fori_loop(0, WIDTH // 64, block, 0)


def load_rows(blocks, rows):
    for s in range(RANKS):
        for u in range(2):
            rows[u, s * CHAN : (s + 1) * CHAN, :] = blocks[s, :, u * 128 : (u + 1) * 128].astype(F32)


def store_rows(rows, blocks):
    for s in range(RANKS):
        for u in range(2):
            blocks[s, :, u * 128 : (u + 1) * 128] = rows[u, s * CHAN : (s + 1) * CHAN, :].astype(BF16)


def partner(e):
    x, y, z, b = coords()
    return device((x + e // 16) % 4, (y + (e // 4) % 4) % 4, (z + (e // 2) % 2) % 2, (b + e % 2) % 2)


def remote(src, dst, there, send_sem, recv_sem):
    return pltpu.make_async_remote_copy(
        src_ref=src, dst_ref=dst, send_sem=send_sem, recv_sem=recv_sem, device_id=there, device_id_type=MESH
    )


def start_exchange(src, got, send_sem, recv_sem):
    me = lax.axis_index("ctx")

    def send(e):
        there = partner(e)
        remote(src.at[there[0]], got.at[me], there, send_sem, recv_sem).start()

    def far(i, carry):
        send((i // 2) * 4 + i % 2 + 2)
        return carry

    def near(i, carry):
        send((i // 2) * 4 + i % 2)
        return carry

    lax.fori_loop(0, 32, far, 0)
    lax.fori_loop(1, 32, near, 0)
    got[me] = src[me]


def finish(blocks, sem):
    others = blocks.at[pl.ds(0, RANKS - 1)]
    pltpu.make_async_copy(others, others, sem).wait()


def kernel(
    in_gate, values, taps, out_gate, shard, out_grad, one, cos_t, sin_t, two_hi, two_lo, last,
    out_gate_grad, got_gg, got_tg, weight_grad,
    src_in, got_g, got_h, src_h, src_c, got_c, src_d, got_d, src_gg, src_tg,
    weights, turned, pair_grad, grad_y,
    rows, z_hi, z_lo, spec, spec_g, spec_h,
    pair_mixed, send_one, recv_one, send_two, recv_two, send_three, recv_three, own,
    ex_send, ex_recv, ag_send, ag_recv, sib_send, sib_recv, rs_send, rs_recv,
):
    x, y, z, b = coords()
    sibling = device(x, y, z, 1 - b)
    tabs = (one, cos_t, sin_t, two_hi, two_lo, last)
    half = WIDTH // 2
    halves = (pl.ds(0, half), pl.ds(half, half))
    sent = []

    barrier = pltpu.get_barrier_semaphore()

    def say(e, carry):
        pl.semaphore_signal(barrier, inc=1, device_id=partner(e), device_id_type=MESH)
        return carry

    lax.fori_loop(1, RANKS, say, 0)
    weights[x, y, z, b] = shard[...]
    for n in range(WIDTH // 128):
        at = slice(n * 128, (n + 1) * 128)
        gated = (in_gate[:, at].astype(F32) * values[:, at].astype(F32)).astype(BF16).astype(F32)
        src_in[n * 8 : (n + 1) * 8] = gated.T.astype(BF16).reshape(8, CHAN, POS)
        src_h[n * 8 : (n + 1) * 8] = taps[:, at].astype(F32).T.astype(BF16).reshape(8, CHAN, POS)
    pl.semaphore_wait(barrier, RANKS - 1)

    def gather(slot, n, there):
        copy = remote(slot, slot, there, ag_send.at[n], ag_recv.at[n])
        copy.start()
        sent.append(copy)
        return copy

    relays = []

    def relay(slot):
        n = len(relays)
        copy = remote(slot, slot, sibling, sib_send.at[n], sib_recv.at[n])
        copy.start()
        sent.append(copy)
        relays.append(copy)

    def first_round(plane, n):
        stage = []
        for d in (2, 1, 3):
            stage.append(gather(weights.at[x, y, plane, b, :, halves[0]], n + d, device((x + d) % 4, y, z, b)))
            stage.append(gather(weights.at[x, y, plane, b, :, halves[1]], n + 3 + d, device(x, (y + d) % 4, z, b)))
        relay(weights.at[x, y, plane, b])
        return stage

    def second_round(plane, n, stage):
        for copy in stage:
            copy.wait_recv()
        stage = []
        for d in (2, 1, 3):
            stage.append(gather(weights.at[:, y, plane, b, :, halves[0]], n + d, device(x, (y + d) % 4, z, b)))
            stage.append(gather(weights.at[x, :, plane, b, :, halves[1]], n + 3 + d, device((x + d) % 4, y, z, b)))
        for d in (2, 1, 3):
            relay(weights.at[(x + 4 - d) % 4, y, plane, b, :, halves[0]])
            relay(weights.at[x, (y + 4 - d) % 4, plane, b, :, halves[1]])
        return stage

    def last_round(plane, stage):
        for n, d in enumerate((2, 1, 3)):
            stage[2 * n].wait_recv()
            relay(weights.at[:, (y + 4 - d) % 4, plane, b, :, halves[0]])
            stage[2 * n + 1].wait_recv()
            relay(weights.at[(x + 4 - d) % 4, :, plane, b, :, halves[1]])

    far = gather(weights.at[x, y, z, b], 0, device(x, y, 1 - z, b))
    near_stage = first_round(z, 0)
    start_exchange(src_in, got_g, ex_send.at[0], ex_recv.at[0])
    start_exchange(src_h, got_h, ex_send.at[1], ex_recv.at[1])
    far.wait_recv()
    far_stage = first_round(1 - z, 6)

    for n in range(MODEL // 128):
        at = slice(n * 128, (n + 1) * 128)
        turned[at, :] = out_grad[:, at].astype(F32).T.astype(BF16)

    near_stage = second_round(z, 12, near_stage)

    def mine(n, carry):
        at = pl.ds(pl.multiple_of(n * 128 + b * 64, 64), 64)
        pair_grad[b, pl.ds(pl.multiple_of(n * 64, 64), 64), :] = turned[at, :]
        return carry

    def theirs(n, carry):
        at = pl.ds(pl.multiple_of(n * 128 + (1 - b) * 64, 64), 64)
        kept = pl.ds(pl.multiple_of(n * 64, 64), 64)
        turned[kept, :] = turned[at, :]
        return carry

    lax.fori_loop(0, MODEL // 128, mine, 0)
    lax.fori_loop(0, MODEL // 128, theirs, 0)
    pair = remote(turned.at[pl.ds(0, MODEL // 2)], pair_grad.at[b], sibling, rs_send.at[14], rs_recv.at[14])
    pair.start()
    sent.append(pair)

    far_stage = second_round(1 - z, 18, far_stage)

    finish(got_g, ex_recv.at[0])
    load_rows(got_g, rows)
    transform(rows, tabs, z_hi, z_lo, spec_g)
    finish(got_h, ex_recv.at[1])
    load_rows(got_h, rows)
    transform(rows, tabs, z_hi, z_lo, spec_h)
    last_round(z, near_stage)
    spectral_product(spec_g, spec_h, False, z_hi, z_lo)
    signal_of(tabs, z_hi, z_lo, spec, rows)
    store_rows(rows, src_c)
    start_exchange(src_c, got_c, ex_send.at[2], ex_recv.at[2])

    last_round(1 - z, far_stage)
    for copy in relays:
        copy.wait_recv()
    for n in range(WIDTH // 256):
        at = slice(n * 256, (n + 1) * 256)
        right = weights[:, :, :, :, :, at].reshape(MODEL, 256)
        product = jnp.dot(out_grad[...], right, preferred_element_type=F32).astype(BF16)
        grad_y[:, at] = product
        grad_conv = (product.astype(F32) * out_gate[:, at].astype(F32)).astype(BF16).astype(F32)
        src_d[n * 16 : (n + 1) * 16] = grad_conv.T.astype(BF16).reshape(16, CHAN, POS)
    start_exchange(src_d, got_d, ex_send.at[3], ex_recv.at[3])

    finish(got_c, ex_recv.at[2])
    for n in range(WIDTH // 128):
        at = slice(n * 128, (n + 1) * 128)
        conv = got_c[n * 8 : (n + 1) * 8].reshape(128, POS).astype(F32).T
        pair_mixed[b, :, at] = (out_gate[:, at].astype(F32) * conv).astype(BF16)
        out_gate_grad[:, at] = (grad_y[:, at].astype(F32) * conv).astype(BF16)
    mixed = remote(pair_mixed.at[b], pair_mixed.at[b], sibling, rs_send.at[0], rs_recv.at[0])
    mixed.start()
    sent.append(mixed)

    def partial(first_row, count, at):
        at_rows = pl.ds(pl.multiple_of(first_row, 128), count)
        return jnp.dot(pair_grad[0, at_rows, :], pair_mixed[0, :, at], preferred_element_type=F32) + jnp.dot(
            pair_grad[1, at_rows, :], pair_mixed[1, :, at], preferred_element_type=F32
        )

    def reduce_to(src, dst, n, there):
        copy = remote(src, dst, there, rs_send.at[n], rs_recv.at[n])
        copy.start()
        sent.append(copy)
        return copy

    pair.wait_recv()
    mixed.wait_recv()
    lanes = (slice(0, half), slice(half, WIDTH))
    stage = []
    for d in (2, 1, 3):
        to = (x + d) % 4
        send_one[0, d - 1] = partial(to * 512, 512, lanes[0]).astype(BF16)
        stage.append(reduce_to(send_one.at[0, d - 1], recv_one.at[0, d - 1], d, device(to, y, z, b)))
        to = (y + d) % 4
        for u in range(4):
            send_one[1, d - 1, u * 128 : (u + 1) * 128, :] = partial(u * 512 + to * 128, 128, lanes[1]).astype(BF16)
        stage.append(reduce_to(send_one.at[1, d - 1], recv_one.at[1, d - 1], 3 + d, device(x, to, z, b)))
    own[0] = partial(x * 512, 512, lanes[0])
    for u in range(4):
        own[1, u * 128 : (u + 1) * 128, :] = partial(u * 512 + y * 128, 128, lanes[1])

    finish(got_d, ex_recv.at[3])
    load_rows(got_d, rows)
    spec_d = spec
    transform(rows, tabs, z_hi, z_lo, spec_d)
    spectral_product(spec_h, spec_d, True, z_hi, z_lo)
    signal_of(tabs, z_hi, z_lo, spec_h, rows)
    store_rows(rows, src_gg)
    start_exchange(src_gg, got_gg, ex_send.at[4], ex_recv.at[4])
    spectral_product(spec_g, spec_d, True, z_hi, z_lo)
    signal_of(tabs, z_hi, z_lo, spec_h, rows)
    store_rows(rows, src_tg)
    start_exchange(src_tg, got_tg, ex_send.at[5], ex_recv.at[5])

    for copy in stage:
        copy.wait_recv()

    def summed(h, place):
        at = pl.ds(pl.multiple_of(place * 128, 128), 128)
        total = own[h, at, :]
        for d in range(3):
            total = total + recv_one[h, d, at, :].astype(F32)
        return total

    stage = []
    for d in (2, 1, 3):
        to = (y + d) % 4
        send_two[0, d - 1] = summed(0, to).astype(BF16)
        stage.append(reduce_to(send_two.at[0, d - 1], recv_two.at[0, d - 1], 6 + d, device(x, to, z, b)))
        to = (x + d) % 4
        send_two[1, d - 1] = summed(1, to).astype(BF16)
        stage.append(reduce_to(send_two.at[1, d - 1], recv_two.at[1, d - 1], 9 + d, device(to, y, z, b)))
    own[0, 0:128, :] = summed(0, y)
    own[1, 0:128, :] = summed(1, x)
    for copy in stage:
        copy.wait_recv()
    for h in range(2):
        total = own[h, 0:128, :]
        for d in range(3):
            total = total + recv_two[h, d].astype(F32)
        own[h, 0:128, :] = total
    there = pl.ds(pl.multiple_of((1 - z) * 64, 64), 64)
    here = pl.ds(pl.multiple_of(z * 64, 64), 64)
    send_three[0] = own[0, there, :].astype(BF16)
    send_three[1] = own[1, there, :].astype(BF16)
    reduce_to(send_three, recv_three, 13, device(x, y, 1 - z, b)).wait_recv()
    for h in range(2):
        weight_grad[:, lanes[h]] = own[h, here, :] + recv_three[h].astype(F32)

    finish(got_gg, ex_recv.at[4])
    finish(got_tg, ex_recv.at[5])
    for n, blocks in enumerate((src_in, src_h, src_c, src_d, src_gg, src_tg)):
        finish(blocks, ex_send.at[n])
    for copy in sent:
        copy.wait_send()


WHOLE = pl.BlockSpec(memory_space=pltpu.VMEM)
DMA = pltpu.SemaphoreType.DMA


def product(left, right):
    return (left.astype(F32) * right.astype(F32)).astype(BF16)


def on_device(out_gate, in_gate, values, filter_taps, out_grad, out_weight):
    tabs = [jnp.asarray(table) for table in tables()]
    shape = jax.ShapeDtypeStruct
    half = WIDTH // 2
    blocks = (RANKS, CHAN, POS)
    operands = (in_gate, values, filter_taps, out_gate, out_weight.T, out_grad, *tabs)
    outs = [shape((POS, WIDTH), BF16), shape(blocks, BF16), shape(blocks, BF16), shape((64, WIDTH), F32)]
    out_gate_grad, got_gg, got_tg, weight_grad = pl.pallas_call(
        kernel,
        name="hyena_backward",
        out_shape=outs,
        in_specs=[WHOLE] * len(operands),
        out_specs=[WHOLE] * len(outs),
        scratch_shapes=[pltpu.VMEM(blocks, BF16) for _ in range(10)]
        + [
            pltpu.VMEM((4, 4, 2, 2, 64, WIDTH), BF16),
            pltpu.VMEM((MODEL, POS), BF16),
            pltpu.VMEM((2, MODEL // 2, POS), BF16),
            pltpu.VMEM((POS, WIDTH), BF16),
            pltpu.VMEM((2, WIDTH, 128), F32),
            pltpu.VMEM((WIDTH, 2 * POS), BF16),
            pltpu.VMEM((WIDTH, 2 * POS), BF16),
            pltpu.VMEM((WIDTH, 2 * POS), F32),
            pltpu.VMEM((WIDTH, 2 * POS), F32),
            pltpu.VMEM((WIDTH, 2 * POS), F32),
            pltpu.VMEM((2, POS, WIDTH), BF16),
            pltpu.VMEM((2, 3, 512, half), BF16),
            pltpu.VMEM((2, 3, 512, half), BF16),
            pltpu.VMEM((2, 3, 128, half), BF16),
            pltpu.VMEM((2, 3, 128, half), BF16),
            pltpu.VMEM((2, 64, half), BF16),
            pltpu.VMEM((2, 64, half), BF16),
            pltpu.VMEM((2, 512, half), F32),
            DMA((6,)),
            DMA((6,)),
            DMA((25,)),
            DMA((25,)),
            DMA((26,)),
            DMA((26,)),
            DMA((15,)),
            DMA((15,)),
        ],
        compiler_params=pltpu.CompilerParams(
            collective_id=0, has_side_effects=True, vmem_limit_bytes=VMEM_LIMIT
        ),
    )(*operands)
    grad_gated = got_gg.reshape(WIDTH, POS).T
    taps_grad = got_tg.reshape(WIDTH, POS).T.astype(F32)
    return (
        out_gate_grad,
        product(grad_gated, values),
        product(grad_gated, in_gate),
        taps_grad,
        weight_grad.T,
    )


def solution(mesh):
    return jax.shard_map(
        on_device,
        mesh=mesh,
        in_specs=(
            P("ctx", "ch"),
            P("ctx", "ch"),
            P("ctx", "ch"),
            P("ctx", "ch"),
            P("ctx", None),
            P("ch", "ctx"),
        ),
        out_specs=(P("ctx", "ch"), P("ctx", "ch"), P("ctx", "ch"), P("ctx", "ch"), P("ch", "ctx")),
        check_vma=False,
    )
```

```python
import functools

import jax
import jax.numpy as jnp
import numpy as np
from jax import lax
from jax.experimental import pallas as pl
from jax.experimental.pallas import tpu as pltpu
from jax.sharding import PartitionSpec as P

MESH = pl.DeviceIdType.MESH
F32 = jnp.float32
BF16 = jnp.bfloat16

RANKS = 64
POS = 256
CHAN = 16
GROUP = CHAN // 2
WIDTH = RANKS * CHAN
MODEL = 4096
VMEM_LIMIT = 60 * 2**20


def coords():
    i = lax.axis_index("ctx")
    return i // 16, (i // 4) % 4, (i // 2) % 2, i % 2


def device(x, y, z, b):
    return (((x * 4 + y) * 2 + z) * 2 + b, lax.axis_index("ch"))


def split(x):
    hi = x.astype(BF16)
    return hi, (x - hi.astype(F32)).astype(BF16)


def tables():
    n = RANKS * POS
    k1 = np.arange(RANKS) + 0.25
    first = 2 * np.pi * k1[:, None] * np.arange(RANKS)[None, :] / RANKS
    turn = 2 * np.pi * k1[:, None] * np.arange(POS)[None, :] / n
    second = 2 * np.pi * ((np.arange(POS)[:, None] * np.arange(POS)[None, :]) % POS) / POS

    def parts(table):
        hi = table.astype(jnp.bfloat16)
        lo = (table - hi.astype(np.float64)).astype(jnp.bfloat16)
        return hi, lo

    one = np.concatenate([np.cos(first), -np.sin(first)], 0)
    one_hi, one_lo = parts(one)
    cos, sin = np.cos(second), np.sin(second)
    two_hi, two_lo = parts(np.block([[cos, -sin], [sin, cos]]))
    last = np.concatenate([np.cos(first), np.sin(first)], 0).T / n
    last_hi, last_lo = parts(last)
    return (
        np.concatenate([one_hi, one_lo], 1),
        np.cos(turn).astype(np.float32),
        (-np.sin(turn)).astype(np.float32),
        two_hi,
        two_lo,
        np.concatenate([last_hi, last_lo, last_hi], 1),
    )


def wide(rows, i):
    return jnp.concatenate([rows[u, pl.ds(i, RANKS, stride=CHAN), :] for u in range(2)], 1)


def narrow(rows, i):
    return jnp.concatenate([rows[pl.ds(u * GROUP + i, RANKS, stride=CHAN), :] for u in range(2)], 1)


def put_wide(rows, i, signal):
    for u in range(2):
        rows[u, pl.ds(i, RANKS, stride=CHAN), :] = signal[:, u * 128 : (u + 1) * 128]


def put_narrow(rows, i, signal):
    for u in range(2):
        rows[pl.ds(u * GROUP + i, RANKS, stride=CHAN), :] = signal[:, u * 128 : (u + 1) * 128]


def turn(re, im, tabs, z_hi, z_lo, i):
    at = slice(i * RANKS, (i + 1) * RANKS)
    cos_t, sin_t = tabs[1][...], tabs[2][...]
    z_hi[at, :POS], z_lo[at, :POS] = split(re * cos_t - im * sin_t)
    z_hi[at, POS:], z_lo[at, POS:] = split(re * sin_t + im * cos_t)


def transform(pick, rows, count, tabs, z_hi, z_lo, spec):
    for i in range(count):
        x = pick(rows, i).astype(BF16)
        a = jnp.dot(tabs[0][...], jnp.concatenate([x, x], 0), preferred_element_type=F32)
        turn(a[:RANKS], a[RANKS:], tabs, z_hi, z_lo, i)
    second(count, tabs, z_hi, z_lo, spec)


def second(count, tabs, z_hi, z_lo, spec):
    _, _, _, two_hi, two_lo, _ = tabs

    def block(i, carry):
        at = pl.ds(pl.multiple_of(i * 256, 256), 256)
        spec[at, :] = (
            jnp.dot(z_hi[at, :], two_hi[...], preferred_element_type=F32)
            + jnp.dot(z_hi[at, :], two_lo[...], preferred_element_type=F32)
            + jnp.dot(z_lo[at, :], two_hi[...], preferred_element_type=F32)
        )
        return carry

    lax.fori_loop(0, count * RANKS // 256, block, 0)


def signals_of(put, rows, count, tabs, z_hi, z_lo, spec):
    second(count, tabs, z_hi, z_lo, spec)
    cos_t, sin_t, last = tabs[1], tabs[2], tabs[5]
    for i in range(count):
        at = slice(i * RANKS, (i + 1) * RANKS)
        re, im = spec[at, :POS], spec[at, POS:]
        hi_re, lo_re = split(re * cos_t[...] - im * sin_t[...])
        hi_im, lo_im = split(re * sin_t[...] + im * cos_t[...])
        stack = jnp.concatenate([hi_re, hi_im, hi_re, hi_im, lo_re, lo_im], 0)
        put(rows, i, jnp.dot(last[...], stack, preferred_element_type=F32))


def spectral_product(left, left_row, right, right_row, conj_right, z_hi, z_lo, row):
    def block(i, carry):
        def at(start):
            return pl.ds(pl.multiple_of(start + i * 64, 64), 64)

        one, two, out = at(left_row), at(right_row), at(row)
        a, b, c, d = left[one, :POS], left[one, POS:], right[two, :POS], right[two, POS:]
        if conj_right:
            re, im = a * c + b * d, b * c - a * d
        else:
            re, im = a * c - b * d, -(a * d + b * c)
        z_hi[out, :POS], z_lo[out, :POS] = split(re)
        z_hi[out, POS:], z_lo[out, POS:] = split(im)
        return carry

    lax.fori_loop(0, GROUP, block, 0)


def load_wide(blocks, g, rows):
    for s in range(RANKS):
        for u in range(2):
            rows[u, s * CHAN : (s + 1) * CHAN, :] = blocks[s, g, :, u * 128 : (u + 1) * 128].astype(F32)


def store_wide(rows, blocks, g):
    for s in range(RANKS):
        for u in range(2):
            blocks[s, g, :, u * 128 : (u + 1) * 128] = rows[u, s * CHAN : (s + 1) * CHAN, :].astype(BF16)


def load_narrow(blocks, g, rows):
    for s in range(RANKS):
        rows[s * CHAN : (s + 1) * CHAN, :] = blocks[s, g].astype(F32)


def store_narrow(rows, blocks, g):
    for s in range(RANKS):
        blocks[s, g] = rows[s * CHAN : (s + 1) * CHAN, :].astype(BF16)


def partner(e):
    x, y, z, b = coords()
    return device((x + e // 16) % 4, (y + (e // 4) % 4) % 4, (z + (e // 2) % 2) % 2, (b + e % 2) % 2)


def remote(src, dst, there, send_sem, recv_sem):
    return pltpu.make_async_remote_copy(
        src_ref=src, dst_ref=dst, send_sem=send_sem, recv_sem=recv_sem, device_id=there, device_id_type=MESH
    )


def start_exchange(src, got, g, send_sem, recv_sem):
    me = lax.axis_index("ctx")

    def send(e):
        there = partner(e)
        remote(src.at[there[0], g], got.at[me, g], there, send_sem, recv_sem).start()

    def far(i, carry):
        send((i // 2) * 4 + i % 2 + 2)
        return carry

    def near(i, carry):
        send((i // 2) * 4 + i % 2)
        return carry

    lax.fori_loop(0, 32, far, 0)
    lax.fori_loop(1, 32, near, 0)
    got[me, g] = src[me, g]


def finish(blocks, g, sem):
    others = blocks.at[pl.ds(0, RANKS - 1), g]
    pltpu.make_async_copy(others, others, sem).wait()


def kernel(
    *refs,
):
    far_refs, (
        out_gate_grad, got_out, weight_grad,
        src_in, got_in, src_out, src_c, got_c, src_d, got_d,
        weights, turned, planes, pair_grad, grad_y,
        rows, short_rows, z_hi, z_lo, spec, spec_0, spec_1, spec_d, product_sum,
        pair_mixed, send_one, recv_hop, recv_one, send_two, recv_two, send_three, recv_three, own,
        ex_send, ex_recv, ag_send, ag_recv, sib_send, sib_recv, rs_send, rs_recv,
        stage_sem, *held_refs,
    ) = refs[:OPERANDS], refs[OPERANDS:]
    staging = [
        pltpu.make_async_copy(source, target, stage_sem.at[n])
        for n, (source, target) in enumerate(zip(far_refs, held_refs))
    ]
    in_gate, values, taps, shard, out_grad, out_gate, one, cos_t, sin_t, two_hi, two_lo, last = held_refs
    for copy in staging:
        copy.start()
    x, y, z, b = coords()
    sibling = device(x, y, z, 1 - b)
    tabs = (one, cos_t, sin_t, two_hi, two_lo, last)
    half = WIDTH // 2
    halves = (pl.ds(0, half), pl.ds(half, half))
    sent = []

    barrier = pltpu.get_barrier_semaphore()

    def say(e, carry):
        pl.semaphore_signal(barrier, inc=1, device_id=partner(e), device_id_type=MESH)
        return carry

    lax.fori_loop(1, RANKS, say, 0)
    for copy in staging[:4]:
        copy.wait()
    weights[x, y, z, b] = shard[...]
    for n in range(WIDTH // 128):
        at = slice(n * 128, (n + 1) * 128)
        gated = (in_gate[:, at].astype(F32) * values[:, at].astype(F32)).astype(BF16).astype(F32)
        both = (gated.T.reshape(8, CHAN, POS), taps[:, at].astype(F32).T.reshape(8, CHAN, POS))
        for g in range(2):
            kept = slice(g * GROUP, (g + 1) * GROUP)
            src_in[n * 8 : (n + 1) * 8, g] = jnp.concatenate([a[:, kept] for a in both], 1).astype(BF16)
    pl.semaphore_wait(barrier, RANKS - 1)

    def gather(slot, n, there):
        copy = remote(slot, slot, there, ag_send.at[n], ag_recv.at[n])
        copy.start()
        sent.append(copy)
        return copy

    relays = []

    def relay(slot):
        n = len(relays)
        copy = remote(slot, slot, sibling, sib_send.at[n], sib_recv.at[n])
        copy.start()
        sent.append(copy)
        relays.append(copy)

    def first_round(plane, n):
        stage = []
        for d in (2, 1, 3):
            stage.append(gather(weights.at[x, y, plane, b, :, halves[0]], n + d, device((x + d) % 4, y, z, b)))
            stage.append(gather(weights.at[x, y, plane, b, :, halves[1]], n + 3 + d, device(x, (y + d) % 4, z, b)))
        relay(weights.at[x, y, plane, b])
        return stage

    def second_round(plane, n, stage):
        for copy in stage:
            copy.wait_recv()
        stage = []
        for d in (1, 3):
            stage.append(gather(weights.at[:, y, plane, b, :, halves[0]], n + d, device(x, (y + d) % 4, z, b)))
            stage.append(gather(weights.at[x, :, plane, b, :, halves[1]], n + 3 + d, device((x + d) % 4, y, z, b)))
        for d in (2, 1, 3):
            relay(weights.at[(x + 4 - d) % 4, y, plane, b, :, halves[0]])
            relay(weights.at[x, (y + 4 - d) % 4, plane, b, :, halves[1]])
        return stage

    def pass_on(plane, n, stage):
        onward = []
        for i, (d, part) in enumerate(((1, pl.ds(0, 32)), (3, pl.ds(32, 32)))):
            stage[2 * i].wait_recv()
            at = (y + 4 - d) % 4
            slot = weights.at[:, at, plane, b, part, halves[0]]
            onward.append(gather(slot, n + 2 * i, device(x, (y + d) % 4, z, b)))
            relay(weights.at[:, at, plane, b, :, halves[0]])
            stage[2 * i + 1].wait_recv()
            at = (x + 4 - d) % 4
            slot = weights.at[at, :, plane, b, part, halves[1]]
            onward.append(gather(slot, n + 2 * i + 1, device((x + d) % 4, y, z, b)))
            relay(weights.at[at, :, plane, b, :, halves[1]])
        return onward

    def last_round(plane, onward):
        for copy in onward:
            copy.wait_recv()
        relay(weights.at[:, (y + 2) % 4, plane, b, :, halves[0]])
        relay(weights.at[(x + 2) % 4, :, plane, b, :, halves[1]])

    far = gather(weights.at[x, y, z, b], 0, device(x, y, 1 - z, b))
    near_stage = first_round(z, 0)
    for g in range(2):
        start_exchange(src_in, got_in, g, ex_send.at[g], ex_recv.at[g])
    far.wait_recv()
    far_stage = first_round(1 - z, 6)

    for copy in staging[4:]:
        copy.wait()
    for n in range(MODEL // 128):
        at = slice(n * 128, (n + 1) * 128)
        turned[at, :] = out_grad[:, at].astype(F32).T.astype(BF16)

    near_stage = second_round(z, 12, near_stage)
    for n in range(16):
        for p in range(2):
            planes[p, :, n * 128 : (n + 1) * 128] = out_grad[:, n * 256 + p * 128 : n * 256 + (p + 1) * 128]

    def mine(n, carry):
        at = pl.ds(pl.multiple_of(n * 128 + b * 64, 64), 64)
        pair_grad[b, pl.ds(pl.multiple_of(n * 64, 64), 64), :] = turned[at, :]
        return carry

    def theirs(n, carry):
        at = pl.ds(pl.multiple_of(n * 128 + (1 - b) * 64, 64), 64)
        kept = pl.ds(pl.multiple_of(n * 64, 64), 64)
        turned[kept, :] = turned[at, :]
        return carry

    lax.fori_loop(0, MODEL // 128, mine, 0)
    lax.fori_loop(0, MODEL // 128, theirs, 0)
    pair = remote(turned.at[pl.ds(0, MODEL // 2)], pair_grad.at[b], sibling, rs_send.at[20], rs_recv.at[20])
    pair.start()
    sent.append(pair)

    far_stage = second_round(1 - z, 18, far_stage)

    specs = (spec_0, spec_1)
    onward = []
    for g, (plane, n, stage) in enumerate(((z, 25, near_stage), (1 - z, 29, far_stage))):
        finish(got_in, g, ex_recv.at[g])
        load_wide(got_in, g, rows)
        if g == 1:
            onward.append(pass_on(plane, n, stage))
        transform(wide, rows, CHAN, tabs, z_hi, z_lo, specs[g])
        if g == 0:
            onward.append(pass_on(plane, n, stage))
        spectral_product(specs[g], 0, specs[g], WIDTH // 2, False, z_hi, z_lo, 0)
        signals_of(put_narrow, short_rows, GROUP, tabs, z_hi, z_lo, spec)
        store_narrow(short_rows, src_c, g)
        start_exchange(src_c, got_c, g, ex_send.at[2 + g], ex_recv.at[2 + g])
    near_onward, far_onward = onward

    def share(plane, at):
        right = weights[:, :, plane, :, :, at].reshape(MODEL // 2, 256)
        return jnp.dot(planes[plane], right, preferred_element_type=F32)

    last_round(z, near_onward)
    last_round(1 - z, far_onward)
    near_relays = relays[:1] + relays[2:8] + relays[14:18] + relays[22:24]
    far_relays = relays[1:2] + relays[8:14] + relays[18:22] + relays[24:26]
    for copy in near_relays:
        copy.wait_recv()
    for n in range(WIDTH // 256):
        at = slice(n * 256, (n + 1) * 256)
        product_sum[:, at] = share(z, at)
    for copy in far_relays:
        copy.wait_recv()
    for n in range(WIDTH // 256):
        at = slice(n * 256, (n + 1) * 256)
        product = (product_sum[:, at] + share(1 - z, at)).astype(BF16)
        grad_y[:, at] = product
        grad_conv = (product.astype(F32) * out_gate[:, at].astype(F32)).astype(BF16).astype(F32)
        grad_conv = grad_conv.T.reshape(16, CHAN, POS)
        for g in range(2):
            kept = grad_conv[:, g * GROUP : (g + 1) * GROUP]
            pair_of = jnp.concatenate([kept[:, :, :128], kept[:, :, 128:]], 1)
            src_d[n * 16 : (n + 1) * 16, g] = pair_of.astype(BF16)
    for g in range(2):
        start_exchange(src_d, got_d, g, ex_send.at[4 + g], ex_recv.at[4 + g])

    for g in range(2):
        finish(got_c, g, ex_recv.at[2 + g])
    for n in range(WIDTH // 128):
        at = slice(n * 128, (n + 1) * 128)
        block = got_c[n * 8 : (n + 1) * 8].astype(F32)
        for u in range(2):
            there = slice(u * 128, (u + 1) * 128)
            conv = block[:, :, u * GROUP : (u + 1) * GROUP].reshape(128, 128).T
            pair_mixed[b, there, at] = (out_gate[there, at].astype(F32) * conv).astype(BF16)
            out_gate_grad[there, at] = (grad_y[there, at].astype(F32) * conv).astype(BF16)
    mixed = remote(pair_mixed.at[b], pair_mixed.at[b], sibling, rs_send.at[0], rs_recv.at[0])
    mixed.start()
    sent.append(mixed)

    def partial(first_row, count, at):
        at_rows = pl.ds(pl.multiple_of(first_row, 128), count)
        left = jnp.concatenate([pair_grad[0, at_rows, :], pair_grad[1, at_rows, :]], 1)
        return jnp.dot(left, pair_mixed[:, :, at].reshape(2 * POS, half), preferred_element_type=F32)

    def reduce_to(src, dst, n, there):
        copy = remote(src, dst, there, rs_send.at[n], rs_recv.at[n])
        copy.start()
        sent.append(copy)
        return copy

    pair.wait_recv()
    mixed.wait_recv()
    lanes = (slice(0, half), slice(half, WIDTH))

    def chunk(h, to, part):
        if h == 0:
            return partial(to * 512 + part * 256, 256, lanes[0])
        two = [partial((2 * part + u) * 512 + to * 128, 128, lanes[1]) for u in range(2)]
        return jnp.concatenate(two, 0)

    def along(h, d):
        return device((x + d) % 4, y, z, b) if h == 0 else device(x, (y + d) % 4, z, b)

    parts = (slice(0, 256), slice(256, 512))
    place = (x, y)
    hops, stage = [], []
    for h in range(2):
        for i, d in enumerate((1, 3)):
            send_one[h, 2, parts[i], :] = chunk(h, (place[h] + 2) % 4, i).astype(BF16)
            hops.append(
                reduce_to(send_one.at[h, 2, pl.ds(i * 256, 256)], recv_hop.at[h, i], 1 + 6 * h + i, along(h, d))
            )
    for h in range(2):
        for i, d in enumerate((1, 3)):
            j = 1 - i
            send_one[h, i, parts[j], :] = chunk(h, (place[h] + d) % 4, j).astype(BF16)
            rows_j = pl.ds(j * 256, 256)
            stage.append(
                reduce_to(send_one.at[h, i, rows_j], recv_one.at[h, i, rows_j], 3 + 6 * h + i, along(h, d))
            )
    for g in range(2):
        finish(got_d, g, ex_recv.at[4 + g])
        load_narrow(got_d, g, short_rows)
        transform(narrow, short_rows, GROUP, tabs, z_hi, z_lo, spec_d)
        spectral_product(specs[g], WIDTH // 2, spec_d, 0, True, z_hi, z_lo, 0)
        spectral_product(specs[g], 0, spec_d, 0, True, z_hi, z_lo, WIDTH // 2)
        signals_of(put_wide, rows, CHAN, tabs, z_hi, z_lo, spec)
        store_wide(rows, src_out, g)
        start_exchange(src_out, got_out, g, ex_send.at[6 + g], ex_recv.at[6 + g])
        if g == 1:
            break
        for h in range(2):
            for i, d in enumerate((1, 3)):
                mine = chunk(h, (place[h] + d) % 4, i)
                hops[2 * h + i].wait_recv()
                send_one[h, i, parts[i], :] = (mine + recv_hop[h, i].astype(F32)).astype(BF16)
                rows_i = pl.ds(i * 256, 256)
                stage.append(
                    reduce_to(send_one.at[h, i, rows_i], recv_one.at[h, i, rows_i], 5 + 6 * h + i, along(h, d))
                )
        for h in range(2):
            for i in range(2):
                own[h, parts[i], :] = chunk(h, place[h], i)
    for copy in stage:
        copy.wait_recv()

    def summed(h, place):
        at = pl.ds(pl.multiple_of(place * 128, 128), 128)
        total = own[h, at, :]
        for d in range(2):
            total = total + recv_one[h, d, at, :].astype(F32)
        return total

    stage = []
    for d in (2, 1, 3):
        to = (y + d) % 4
        send_two[0, d - 1] = summed(0, to).astype(BF16)
        stage.append(reduce_to(send_two.at[0, d - 1], recv_two.at[0, d - 1], 12 + d, device(x, to, z, b)))
        to = (x + d) % 4
        send_two[1, d - 1] = summed(1, to).astype(BF16)
        stage.append(reduce_to(send_two.at[1, d - 1], recv_two.at[1, d - 1], 15 + d, device(to, y, z, b)))
    own[0, 0:128, :] = summed(0, y)
    own[1, 0:128, :] = summed(1, x)
    for copy in stage:
        copy.wait_recv()
    for h in range(2):
        total = own[h, 0:128, :]
        for d in range(3):
            total = total + recv_two[h, d].astype(F32)
        own[h, 0:128, :] = total
    there = pl.ds(pl.multiple_of((1 - z) * 64, 64), 64)
    here = pl.ds(pl.multiple_of(z * 64, 64), 64)
    send_three[0] = own[0, there, :].astype(BF16)
    send_three[1] = own[1, there, :].astype(BF16)
    reduce_to(send_three, recv_three, 19, device(x, y, 1 - z, b)).wait_recv()
    for h in range(2):
        weight_grad[:, lanes[h]] = own[h, here, :] + recv_three[h].astype(F32)

    for g in range(2):
        finish(got_out, g, ex_recv.at[6 + g])
    for n, blocks in enumerate((src_in, src_c, src_d, src_out)):
        for g in range(2):
            finish(blocks, g, ex_send.at[2 * n + g])
    for copy in sent:
        copy.wait_send()


def last_products(
    blocks, in_gate, values, out_gate_in, weight_in, out_gate_grad, in_gate_grad, values_grad, taps_grad, weight_grad
):
    for n in range(2):
        at = slice(n * 128, (n + 1) * 128)
        block = blocks[n * 8 : (n + 1) * 8].astype(F32)
        grad_gated = block[:, :, :GROUP].reshape(128, POS).T
        in_gate_grad[:, at] = (grad_gated * values[:, at].astype(F32)).astype(BF16)
        values_grad[:, at] = (grad_gated * in_gate[:, at].astype(F32)).astype(BF16)
        taps_grad[:, at] = block[:, :, GROUP:].reshape(128, POS).T
    out_gate_grad[...] = out_gate_in[...]
    weight_grad[...] = weight_in[...]


OPERANDS = 12
WHOLE = pl.BlockSpec(memory_space=pltpu.VMEM)
DMA = pltpu.SemaphoreType.DMA


def on_device(out_gate, in_gate, values, filter_taps, out_grad, out_weight):
    tabs = [jnp.asarray(table) for table in tables()]
    shape = jax.ShapeDtypeStruct
    half = WIDTH // 2
    operands = (in_gate, values, filter_taps, out_weight.T, out_grad, out_gate, *tabs)
    outs = [shape((POS, WIDTH), BF16), shape((RANKS, 2, CHAN, POS), BF16), shape((64, WIDTH), F32)]
    out_gate_grad, got_out, weight_grad = pl.pallas_call(
        kernel,
        name="hyena_backward",
        out_shape=outs,
        in_specs=[pl.BlockSpec(memory_space=pl.ANY)] * len(operands),
        out_specs=[WHOLE] * len(outs),
        scratch_shapes=[pltpu.VMEM((RANKS, 2, CHAN, POS), BF16) for _ in range(3)]
        + [pltpu.VMEM((RANKS, 2, CHAN, 128), BF16) for _ in range(4)]
        + [
            pltpu.VMEM((4, 4, 2, 2, 64, WIDTH), BF16),
            pltpu.VMEM((MODEL, POS), BF16),
            pltpu.VMEM((2, POS, MODEL // 2), BF16),
            pltpu.VMEM((2, MODEL // 2, POS), BF16),
            pltpu.VMEM((POS, WIDTH), BF16),
            pltpu.VMEM((2, WIDTH, 128), F32),
            pltpu.VMEM((WIDTH, 128), F32),
            pltpu.VMEM((WIDTH, 2 * POS), BF16),
            pltpu.VMEM((WIDTH, 2 * POS), BF16),
            pltpu.VMEM((WIDTH, 2 * POS), F32),
            pltpu.VMEM((WIDTH, 2 * POS), F32),
            pltpu.VMEM((WIDTH, 2 * POS), F32),
            pltpu.VMEM((WIDTH // 2, 2 * POS), F32),
            pltpu.VMEM((POS, WIDTH), F32),
            pltpu.VMEM((2, POS, WIDTH), BF16),
            pltpu.VMEM((2, 3, 512, half), BF16),
            pltpu.VMEM((2, 2, 256, half), BF16),
            pltpu.VMEM((2, 2, 512, half), BF16),
            pltpu.VMEM((2, 3, 128, half), BF16),
            pltpu.VMEM((2, 3, 128, half), BF16),
            pltpu.VMEM((2, 64, half), BF16),
            pltpu.VMEM((2, 64, half), BF16),
            pltpu.VMEM((2, 512, half), F32),
            DMA((8,)),
            DMA((8,)),
            DMA((33,)),
            DMA((33,)),
            DMA((26,)),
            DMA((26,)),
            DMA((21,)),
            DMA((21,)),
            DMA((OPERANDS,)),
        ]
        + [pltpu.VMEM(a.shape, a.dtype) for a in operands],
        compiler_params=pltpu.CompilerParams(
            collective_id=0, has_side_effects=True, vmem_limit_bytes=VMEM_LIMIT
        ),
    )(*operands)
    wide_block = pl.BlockSpec((POS, 256), lambda n: (0, n))
    *grads, weight_grad = pl.pallas_call(
        last_products,
        name="last_products",
        grid=(WIDTH // 256,),
        out_shape=[shape((POS, WIDTH), BF16)] * 3 + [shape((POS, WIDTH), F32), shape((64, WIDTH), F32)],
        in_specs=[
            pl.BlockSpec((16, 2, CHAN, POS), lambda n: (n, 0, 0, 0)),
            wide_block,
            wide_block,
            wide_block,
            pl.BlockSpec((64, 256), lambda n: (0, n)),
        ],
        out_specs=[wide_block] * 4 + [pl.BlockSpec((64, 256), lambda n: (0, n))],
    )(got_out, in_gate, values, out_gate_grad, weight_grad)
    return (*grads, weight_grad.T)


def solution(mesh):
    return jax.shard_map(
        on_device,
        mesh=mesh,
        in_specs=(
            P("ctx", "ch"),
            P("ctx", "ch"),
            P("ctx", "ch"),
            P("ctx", "ch"),
            P("ctx", None),
            P("ch", "ctx"),
        ),
        out_specs=(P("ctx", "ch"), P("ctx", "ch"), P("ctx", "ch"), P("ctx", "ch"), P("ch", "ctx")),
        check_vma=False,
    )
```

```python
import functools

import jax
import jax.numpy as jnp
import numpy as np
from jax import lax
from jax.experimental import pallas as pl
from jax.experimental.pallas import tpu as pltpu
from jax.sharding import PartitionSpec as P

MESH = pl.DeviceIdType.MESH
F32 = jnp.float32
BF16 = jnp.bfloat16

RANKS = 64
POS = 256
CHAN = 16
GROUP = CHAN // 2
WIDTH = RANKS * CHAN
MODEL = 4096
VMEM_LIMIT = 60 * 2**20


def coords():
    i = lax.axis_index("ctx")
    return i // 16, (i // 4) % 4, (i // 2) % 2, i % 2


def device(x, y, z, b):
    return (((x * 4 + y) * 2 + z) * 2 + b, lax.axis_index("ch"))


def split(x):
    hi = x.astype(BF16)
    return hi, (x - hi.astype(F32)).astype(BF16)


def tables():
    n = RANKS * POS
    k1 = np.arange(RANKS) + 0.25
    first = 2 * np.pi * k1[:, None] * np.arange(RANKS)[None, :] / RANKS
    turn = 2 * np.pi * k1[:, None] * np.arange(POS)[None, :] / n
    second = 2 * np.pi * ((np.arange(POS)[:, None] * np.arange(POS)[None, :]) % POS) / POS

    def parts(table):
        hi = table.astype(jnp.bfloat16)
        lo = (table - hi.astype(np.float64)).astype(jnp.bfloat16)
        return hi, lo

    one = np.concatenate([np.cos(first), -np.sin(first)], 0)
    one_hi, one_lo = parts(one)
    cos, sin = np.cos(second), np.sin(second)
    two_hi, two_lo = parts(np.block([[cos, -sin], [sin, cos]]))
    last = np.concatenate([np.cos(first), np.sin(first)], 0).T / n
    last_hi, last_lo = parts(last)
    return (
        np.concatenate([one_hi, one_lo], 1),
        np.cos(turn).astype(np.float32),
        (-np.sin(turn)).astype(np.float32),
        two_hi,
        two_lo,
        np.concatenate([last_hi, last_lo, last_hi], 1),
    )


def wide(rows, i):
    return jnp.concatenate([rows[u, pl.ds(i, RANKS, stride=CHAN), :] for u in range(2)], 1)


def narrow(rows, i):
    return jnp.concatenate([rows[pl.ds(u * GROUP + i, RANKS, stride=CHAN), :] for u in range(2)], 1)


def put_wide(rows, i, signal):
    for u in range(2):
        rows[u, pl.ds(i, RANKS, stride=CHAN), :] = signal[:, u * 128 : (u + 1) * 128]


def put_narrow(rows, i, signal):
    for u in range(2):
        rows[pl.ds(u * GROUP + i, RANKS, stride=CHAN), :] = signal[:, u * 128 : (u + 1) * 128]


def turn(re, im, tabs, z_hi, z_lo, i):
    at = slice(i * RANKS, (i + 1) * RANKS)
    cos_t, sin_t = tabs[1][...], tabs[2][...]
    z_hi[at, :POS], z_lo[at, :POS] = split(re * cos_t - im * sin_t)
    z_hi[at, POS:], z_lo[at, POS:] = split(re * sin_t + im * cos_t)


def transform(pick, rows, count, tabs, z_hi, z_lo, spec):
    for i in range(count):
        x = pick(rows, i).astype(BF16)
        a = jnp.dot(tabs[0][...], jnp.concatenate([x, x], 0), preferred_element_type=F32)
        turn(a[:RANKS], a[RANKS:], tabs, z_hi, z_lo, i)
    second(count, tabs, z_hi, z_lo, spec)


def second(count, tabs, z_hi, z_lo, spec):
    _, _, _, two_hi, two_lo, _ = tabs

    def block(i, carry):
        at = pl.ds(pl.multiple_of(i * 256, 256), 256)
        total = jnp.dot(z_hi[at, :], two_hi[...], preferred_element_type=F32) + jnp.dot(
            z_hi[at, :], two_lo[...], preferred_element_type=F32
        )
        if z_lo is not None:
            total = total + jnp.dot(z_lo[at, :], two_hi[...], preferred_element_type=F32)
        spec[at, :] = total
        return carry

    lax.fori_loop(0, count * RANKS // 256, block, 0)


def signals_of(put, rows, count, tabs, z_hi, spec):
    second(count, tabs, z_hi, None, spec)
    cos_t, sin_t, last = tabs[1], tabs[2], tabs[5]
    for i in range(count):
        at = slice(i * RANKS, (i + 1) * RANKS)
        re, im = spec[at, :POS], spec[at, POS:]
        hi_re, lo_re = split(re * cos_t[...] - im * sin_t[...])
        hi_im, lo_im = split(re * sin_t[...] + im * cos_t[...])
        stack = jnp.concatenate([hi_re, hi_im, hi_re, hi_im, lo_re, lo_im], 0)
        put(rows, i, jnp.dot(last[...], stack, preferred_element_type=F32))


def spectral_product(left, left_row, right, right_row, conj_right, z, row):
    def block(i, carry):
        def at(start):
            return pl.ds(pl.multiple_of(start + i * 64, 64), 64)

        one, two, out = at(left_row), at(right_row), at(row)
        a, b, c, d = left[one, :POS], left[one, POS:], right[two, :POS], right[two, POS:]
        if conj_right:
            re, im = a * c + b * d, b * c - a * d
        else:
            re, im = a * c - b * d, -(a * d + b * c)
        z[out, :POS] = re.astype(BF16)
        z[out, POS:] = im.astype(BF16)
        return carry

    lax.fori_loop(0, GROUP, block, 0)


def load_wide(blocks, g, rows):
    for s in range(RANKS):
        for u in range(2):
            rows[u, s * CHAN : (s + 1) * CHAN, :] = blocks[s, g, :, u * 128 : (u + 1) * 128].astype(F32)


def store_wide(rows, blocks, g):
    for s in range(RANKS):
        for u in range(2):
            blocks[s, g, :, u * 128 : (u + 1) * 128] = rows[u, s * CHAN : (s + 1) * CHAN, :].astype(BF16)


def load_narrow(blocks, g, rows):
    for s in range(RANKS):
        rows[s * CHAN : (s + 1) * CHAN, :] = blocks[s, g].astype(F32)


def store_narrow(rows, blocks, g):
    for s in range(RANKS):
        blocks[s, g] = rows[s * CHAN : (s + 1) * CHAN, :].astype(BF16)


def partner(e):
    return (lax.rem(lax.axis_index("ctx") + e, RANKS), lax.axis_index("ch"))


def remote(src, dst, there, send_sem, recv_sem):
    return pltpu.make_async_remote_copy(
        src_ref=src, dst_ref=dst, send_sem=send_sem, recv_sem=recv_sem, device_id=there, device_id_type=MESH
    )


def start_exchange(src, got, g, send_sem, recv_sem):
    me = lax.axis_index("ctx")

    def send(e):
        there = partner(e)
        remote(src.at[there[0], g], got.at[me, g], there, send_sem, recv_sem).start()

    for r in (2, 1, 3, 0):

        def group(i, carry):
            send(4 * i + r)
            return carry

        lax.fori_loop(1 if r == 0 else 0, RANKS // 4, group, 0, unroll=True)
    got[me, g] = src[me, g]


def finish(blocks, g, sem):
    others = blocks.at[pl.ds(0, RANKS - 1), g]
    pltpu.make_async_copy(others, others, sem).wait()


def kernel(
    *refs,
):
    far_refs, (
        out_gate_grad, got_out, weight_grad,
        src_in, got_in, src_out, src_c, got_c, src_d, got_d,
        weights, turned, planes, pair_grad, grad_y,
        rows, short_rows, z_hi, z_lo, spec, spec_0, spec_1, spec_d, product_sum,
        pair_mixed, send_one, recv_hop, recv_one, send_two, recv_two, send_three, recv_three, own,
        ex_send, ex_recv, ag_send, ag_recv, sib_send, sib_recv, rs_send, rs_recv,
        stage_sem, *held_refs,
    ) = refs[:OPERANDS], refs[OPERANDS:]
    staging = [
        pltpu.make_async_copy(source, target, stage_sem.at[n])
        for n, (source, target) in enumerate(zip(far_refs, held_refs))
    ]
    in_gate, values, taps, shard, out_grad, out_gate, one, cos_t, sin_t, two_hi, two_lo, last = held_refs
    for copy in staging:
        copy.start()
    x, y, z, b = coords()
    sibling = device(x, y, z, 1 - b)
    tabs = (one, cos_t, sin_t, two_hi, two_lo, last)
    half = WIDTH // 2
    halves = (pl.ds(0, half), pl.ds(half, half))
    sent = []

    barrier = pltpu.get_barrier_semaphore()

    def say(e, carry):
        pl.semaphore_signal(barrier, inc=1, device_id=partner(e), device_id_type=MESH)
        return carry

    lax.fori_loop(1, RANKS, say, 0, unroll=9)
    for copy in staging[:4]:
        copy.wait()
    weights[x, y, z, b] = shard[...]
    for n in range(WIDTH // 128):
        at = slice(n * 128, (n + 1) * 128)
        gated = (in_gate[:, at].astype(F32) * values[:, at].astype(F32)).astype(BF16).astype(F32)
        both = (gated.T.reshape(8, CHAN, POS), taps[:, at].astype(F32).T.reshape(8, CHAN, POS))
        for g in range(2):
            kept = slice(g * GROUP, (g + 1) * GROUP)
            src_in[n * 8 : (n + 1) * 8, g] = jnp.concatenate([a[:, kept] for a in both], 1).astype(BF16)
    pl.semaphore_wait(barrier, RANKS - 1)

    def gather(slot, n, there):
        copy = remote(slot, slot, there, ag_send.at[n], ag_recv.at[n])
        copy.start()
        sent.append(copy)
        return copy

    relays = []

    def relay(slot):
        n = len(relays)
        copy = remote(slot, slot, sibling, sib_send.at[n], sib_recv.at[n])
        copy.start()
        sent.append(copy)
        relays.append(copy)

    def first_round(plane, n):
        stage = []
        for d in (2, 1, 3):
            stage.append(gather(weights.at[x, y, plane, b, :, halves[0]], n + d, device((x + d) % 4, y, z, b)))
            stage.append(gather(weights.at[x, y, plane, b, :, halves[1]], n + 3 + d, device(x, (y + d) % 4, z, b)))
        relay(weights.at[x, y, plane, b])
        return stage

    def second_round(plane, n, stage):
        for copy in stage:
            copy.wait_recv()
        stage = []
        for d in (1, 3):
            stage.append(gather(weights.at[:, y, plane, b, :, halves[0]], n + d, device(x, (y + d) % 4, z, b)))
            stage.append(gather(weights.at[x, :, plane, b, :, halves[1]], n + 3 + d, device((x + d) % 4, y, z, b)))
        for d in (2, 1, 3):
            relay(weights.at[(x + 4 - d) % 4, y, plane, b, :, halves[0]])
            relay(weights.at[x, (y + 4 - d) % 4, plane, b, :, halves[1]])
        return stage

    def pass_on(plane, n, stage):
        onward = []
        for i, (d, part) in enumerate(((1, pl.ds(0, 32)), (3, pl.ds(32, 32)))):
            stage[2 * i].wait_recv()
            at = (y + 4 - d) % 4
            slot = weights.at[:, at, plane, b, part, halves[0]]
            onward.append(gather(slot, n + 2 * i, device(x, (y + d) % 4, z, b)))
            relay(weights.at[:, at, plane, b, :, halves[0]])
            stage[2 * i + 1].wait_recv()
            at = (x + 4 - d) % 4
            slot = weights.at[at, :, plane, b, part, halves[1]]
            onward.append(gather(slot, n + 2 * i + 1, device((x + d) % 4, y, z, b)))
            relay(weights.at[at, :, plane, b, :, halves[1]])
        return onward

    def last_round(plane, onward):
        for copy in onward:
            copy.wait_recv()
        relay(weights.at[:, (y + 2) % 4, plane, b, :, halves[0]])
        relay(weights.at[(x + 2) % 4, :, plane, b, :, halves[1]])

    far = gather(weights.at[x, y, z, b], 0, device(x, y, 1 - z, b))
    near_stage = first_round(z, 0)
    for g in range(2):
        start_exchange(src_in, got_in, g, ex_send.at[g], ex_recv.at[g])
    far.wait_recv()
    far_stage = first_round(1 - z, 6)

    for copy in staging[4:]:
        copy.wait()
    for n in range(MODEL // 128):
        at = slice(n * 128, (n + 1) * 128)
        turned[at, :] = out_grad[:, at].astype(F32).T.astype(BF16)

    near_stage = second_round(z, 12, near_stage)
    for n in range(16):
        for p in range(2):
            planes[p, :, n * 128 : (n + 1) * 128] = out_grad[:, n * 256 + p * 128 : n * 256 + (p + 1) * 128]

    def mine(n, carry):
        at = pl.ds(pl.multiple_of(n * 128 + b * 64, 64), 64)
        pair_grad[b, pl.ds(pl.multiple_of(n * 64, 64), 64), :] = turned[at, :]
        return carry

    def theirs(n, carry):
        at = pl.ds(pl.multiple_of(n * 128 + (1 - b) * 64, 64), 64)
        kept = pl.ds(pl.multiple_of(n * 64, 64), 64)
        turned[kept, :] = turned[at, :]
        return carry

    lax.fori_loop(0, MODEL // 128, mine, 0)
    lax.fori_loop(0, MODEL // 128, theirs, 0)
    pair = remote(turned.at[pl.ds(0, MODEL // 2)], pair_grad.at[b], sibling, rs_send.at[20], rs_recv.at[20])
    pair.start()
    sent.append(pair)

    far_stage = second_round(1 - z, 18, far_stage)

    specs = (spec_0, spec_1)
    onward = []
    for g, (plane, n, stage) in enumerate(((z, 25, near_stage), (1 - z, 29, far_stage))):
        finish(got_in, g, ex_recv.at[g])
        load_wide(got_in, g, rows)
        if g == 1:
            onward.append(pass_on(plane, n, stage))
        transform(wide, rows, CHAN, tabs, z_hi, z_lo, specs[g])
        if g == 0:
            onward.append(pass_on(plane, n, stage))
        spectral_product(specs[g], 0, specs[g], WIDTH // 2, False, z_hi, 0)
        signals_of(put_narrow, short_rows, GROUP, tabs, z_hi, spec)
        store_narrow(short_rows, src_c, g)
        start_exchange(src_c, got_c, g, ex_send.at[2 + g], ex_recv.at[2 + g])
    near_onward, far_onward = onward

    def share(plane, at):
        right = weights[:, :, plane, :, :, at].reshape(MODEL // 2, 256)
        return jnp.dot(planes[plane], right, preferred_element_type=F32)

    last_round(z, near_onward)
    near_relays = relays[:1] + relays[2:8] + relays[14:18] + relays[22:24]
    for copy in near_relays:
        copy.wait_recv()
    for n in range(WIDTH // 256):
        at = slice(n * 256, (n + 1) * 256)
        product_sum[:, at] = share(z, at)
    last_round(1 - z, far_onward)
    for copy in relays[1:2] + relays[8:14] + relays[18:22] + relays[24:26]:
        copy.wait_recv()
    for n in range(WIDTH // 256):
        at = slice(n * 256, (n + 1) * 256)
        product = (product_sum[:, at] + share(1 - z, at)).astype(BF16)
        grad_y[:, at] = product
        grad_conv = (product.astype(F32) * out_gate[:, at].astype(F32)).astype(BF16).astype(F32)
        grad_conv = grad_conv.T.reshape(16, CHAN, POS)
        for g in range(2):
            kept = grad_conv[:, g * GROUP : (g + 1) * GROUP]
            pair_of = jnp.concatenate([kept[:, :, :128], kept[:, :, 128:]], 1)
            src_d[n * 16 : (n + 1) * 16, g] = pair_of.astype(BF16)
    for g in range(2):
        start_exchange(src_d, got_d, g, ex_send.at[4 + g], ex_recv.at[4 + g])

    for g in range(2):
        finish(got_c, g, ex_recv.at[2 + g])
    for n in range(WIDTH // 128):
        at = slice(n * 128, (n + 1) * 128)
        block = got_c[n * 8 : (n + 1) * 8].astype(F32)
        for u in range(2):
            there = slice(u * 128, (u + 1) * 128)
            conv = block[:, :, u * GROUP : (u + 1) * GROUP].reshape(128, 128).T
            pair_mixed[b, there, at] = (out_gate[there, at].astype(F32) * conv).astype(BF16)
            out_gate_grad[there, at] = (grad_y[there, at].astype(F32) * conv).astype(BF16)
    mixed = remote(pair_mixed.at[b], pair_mixed.at[b], sibling, rs_send.at[0], rs_recv.at[0])
    mixed.start()
    sent.append(mixed)

    def partial(first_row, count, at):
        at_rows = pl.ds(pl.multiple_of(first_row, 128), count)
        left = jnp.concatenate([pair_grad[0, at_rows, :], pair_grad[1, at_rows, :]], 1)
        return jnp.dot(left, pair_mixed[:, :, at].reshape(2 * POS, half), preferred_element_type=F32)

    def reduce_to(src, dst, n, there):
        copy = remote(src, dst, there, rs_send.at[n], rs_recv.at[n])
        copy.start()
        sent.append(copy)
        return copy

    pair.wait_recv()
    mixed.wait_recv()
    lanes = (slice(0, half), slice(half, WIDTH))

    def chunk(h, to, part):
        if h == 0:
            return partial(to * 512 + part * 256, 256, lanes[0])
        two = [partial((2 * part + u) * 512 + to * 128, 128, lanes[1]) for u in range(2)]
        return jnp.concatenate(two, 0)

    def along(h, d):
        return device((x + d) % 4, y, z, b) if h == 0 else device(x, (y + d) % 4, z, b)

    parts = (slice(0, 256), slice(256, 512))
    place = (x, y)
    hops, stage = [], []
    for h in range(2):
        for i, d in enumerate((1, 3)):
            send_one[h, 2, parts[i], :] = chunk(h, (place[h] + 2) % 4, i).astype(BF16)
            hops.append(
                reduce_to(send_one.at[h, 2, pl.ds(i * 256, 256)], recv_hop.at[h, i], 1 + 6 * h + i, along(h, d))
            )
    for h in range(2):
        for i, d in enumerate((1, 3)):
            j = 1 - i
            send_one[h, i, parts[j], :] = chunk(h, (place[h] + d) % 4, j).astype(BF16)
            rows_j = pl.ds(j * 256, 256)
            stage.append(
                reduce_to(send_one.at[h, i, rows_j], recv_one.at[h, i, rows_j], 3 + 6 * h + i, along(h, d))
            )
    for g in range(2):
        finish(got_d, g, ex_recv.at[4 + g])
        load_narrow(got_d, g, short_rows)
        transform(narrow, short_rows, GROUP, tabs, z_hi, z_lo, spec_d)
        spectral_product(specs[g], WIDTH // 2, spec_d, 0, True, z_hi, 0)
        spectral_product(specs[g], 0, spec_d, 0, True, z_hi, WIDTH // 2)
        signals_of(put_wide, rows, CHAN, tabs, z_hi, spec)
        store_wide(rows, src_out, g)
        start_exchange(src_out, got_out, g, ex_send.at[6 + g], ex_recv.at[6 + g])
        if g == 1:
            break
        for h in range(2):
            for i, d in enumerate((1, 3)):
                mine = chunk(h, (place[h] + d) % 4, i)
                hops[2 * h + i].wait_recv()
                send_one[h, i, parts[i], :] = (mine + recv_hop[h, i].astype(F32)).astype(BF16)
                rows_i = pl.ds(i * 256, 256)
                stage.append(
                    reduce_to(send_one.at[h, i, rows_i], recv_one.at[h, i, rows_i], 5 + 6 * h + i, along(h, d))
                )
        for h in range(2):
            for i in range(2):
                own[h, parts[i], :] = chunk(h, place[h], i)
    for copy in stage:
        copy.wait_recv()

    def summed(h, place):
        at = pl.ds(pl.multiple_of(place * 128, 128), 128)
        total = own[h, at, :]
        for d in range(2):
            total = total + recv_one[h, d, at, :].astype(F32)
        return total

    stage = []
    for d in (2, 1, 3):
        to = (y + d) % 4
        send_two[0, d - 1] = summed(0, to).astype(BF16)
        stage.append(reduce_to(send_two.at[0, d - 1], recv_two.at[0, d - 1], 12 + d, device(x, to, z, b)))
        to = (x + d) % 4
        send_two[1, d - 1] = summed(1, to).astype(BF16)
        stage.append(reduce_to(send_two.at[1, d - 1], recv_two.at[1, d - 1], 15 + d, device(to, y, z, b)))
    own[0, 0:128, :] = summed(0, y)
    own[1, 0:128, :] = summed(1, x)
    for copy in stage:
        copy.wait_recv()
    for h in range(2):
        total = own[h, 0:128, :]
        for d in range(3):
            total = total + recv_two[h, d].astype(F32)
        own[h, 0:128, :] = total
    there = pl.ds(pl.multiple_of((1 - z) * 64, 64), 64)
    here = pl.ds(pl.multiple_of(z * 64, 64), 64)
    send_three[0] = own[0, there, :].astype(BF16)
    send_three[1] = own[1, there, :].astype(BF16)
    reduce_to(send_three, recv_three, 19, device(x, y, 1 - z, b)).wait_recv()
    for h in range(2):
        weight_grad[:, lanes[h]] = own[h, here, :] + recv_three[h].astype(F32)

    for g in range(2):
        finish(got_out, g, ex_recv.at[6 + g])
    for n, blocks in enumerate((src_in, src_c, src_d, src_out)):
        for g in range(2):
            finish(blocks, g, ex_send.at[2 * n + g])
    for copy in sent:
        copy.wait_send()


def last_products(
    blocks, in_gate, values, out_gate_in, weight_in, out_gate_grad, in_gate_grad, values_grad, taps_grad, weight_grad
):
    for n in range(2):
        at = slice(n * 128, (n + 1) * 128)
        block = blocks[n * 8 : (n + 1) * 8].astype(F32)
        grad_gated = block[:, :, :GROUP].reshape(128, POS).T
        in_gate_grad[:, at] = (grad_gated * values[:, at].astype(F32)).astype(BF16)
        values_grad[:, at] = (grad_gated * in_gate[:, at].astype(F32)).astype(BF16)
        taps_grad[:, at] = block[:, :, GROUP:].reshape(128, POS).T
    out_gate_grad[...] = out_gate_in[...]
    weight_grad[...] = weight_in[...]


OPERANDS = 12
WHOLE = pl.BlockSpec(memory_space=pltpu.VMEM)
DMA = pltpu.SemaphoreType.DMA


def on_device(out_gate, in_gate, values, filter_taps, out_grad, out_weight):
    tabs = [jnp.asarray(table) for table in tables()]
    shape = jax.ShapeDtypeStruct
    half = WIDTH // 2
    operands = (in_gate, values, filter_taps, out_weight.T, out_grad, out_gate, *tabs)
    outs = [shape((POS, WIDTH), BF16), shape((RANKS, 2, CHAN, POS), BF16), shape((64, WIDTH), F32)]
    out_gate_grad, got_out, weight_grad = pl.pallas_call(
        kernel,
        name="hyena_backward",
        out_shape=outs,
        in_specs=[pl.BlockSpec(memory_space=pl.ANY)] * len(operands),
        out_specs=[WHOLE] * len(outs),
        scratch_shapes=[pltpu.VMEM((RANKS, 2, CHAN, POS), BF16) for _ in range(3)]
        + [pltpu.VMEM((RANKS, 2, CHAN, 128), BF16) for _ in range(4)]
        + [
            pltpu.VMEM((4, 4, 2, 2, 64, WIDTH), BF16),
            pltpu.VMEM((MODEL, POS), BF16),
            pltpu.VMEM((2, POS, MODEL // 2), BF16),
            pltpu.VMEM((2, MODEL // 2, POS), BF16),
            pltpu.VMEM((POS, WIDTH), BF16),
            pltpu.VMEM((2, WIDTH, 128), F32),
            pltpu.VMEM((WIDTH, 128), F32),
            pltpu.VMEM((WIDTH, 2 * POS), BF16),
            pltpu.VMEM((WIDTH, 2 * POS), BF16),
            pltpu.VMEM((WIDTH, 2 * POS), F32),
            pltpu.VMEM((WIDTH, 2 * POS), F32),
            pltpu.VMEM((WIDTH, 2 * POS), F32),
            pltpu.VMEM((WIDTH // 2, 2 * POS), F32),
            pltpu.VMEM((POS, WIDTH), F32),
            pltpu.VMEM((2, POS, WIDTH), BF16),
            pltpu.VMEM((2, 3, 512, half), BF16),
            pltpu.VMEM((2, 2, 256, half), BF16),
            pltpu.VMEM((2, 2, 512, half), BF16),
            pltpu.VMEM((2, 3, 128, half), BF16),
            pltpu.VMEM((2, 3, 128, half), BF16),
            pltpu.VMEM((2, 64, half), BF16),
            pltpu.VMEM((2, 64, half), BF16),
            pltpu.VMEM((2, 512, half), F32),
            DMA((8,)),
            DMA((8,)),
            DMA((33,)),
            DMA((33,)),
            DMA((26,)),
            DMA((26,)),
            DMA((21,)),
            DMA((21,)),
            DMA((OPERANDS,)),
        ]
        + [pltpu.VMEM(a.shape, a.dtype) for a in operands],
        compiler_params=pltpu.CompilerParams(
            collective_id=0, has_side_effects=True, vmem_limit_bytes=VMEM_LIMIT
        ),
    )(*operands)
    wide_block = pl.BlockSpec((POS, 256), lambda n: (0, n))
    *grads, weight_grad = pl.pallas_call(
        last_products,
        name="last_products",
        grid=(WIDTH // 256,),
        out_shape=[shape((POS, WIDTH), BF16)] * 3 + [shape((POS, WIDTH), F32), shape((64, WIDTH), F32)],
        in_specs=[
            pl.BlockSpec((16, 2, CHAN, POS), lambda n: (n, 0, 0, 0)),
            wide_block,
            wide_block,
            wide_block,
            pl.BlockSpec((64, 256), lambda n: (0, n)),
        ],
        out_specs=[wide_block] * 4 + [pl.BlockSpec((64, 256), lambda n: (0, n))],
    )(got_out, in_gate, values, out_gate_grad, weight_grad)
    return (*grads, weight_grad.T)


def solution(mesh):
    return jax.shard_map(
        on_device,
        mesh=mesh,
        in_specs=(
            P("ctx", "ch"),
            P("ctx", "ch"),
            P("ctx", "ch"),
            P("ctx", "ch"),
            P("ctx", None),
            P("ch", "ctx"),
        ),
        out_specs=(P("ctx", "ch"), P("ctx", "ch"), P("ctx", "ch"), P("ctx", "ch"), P("ch", "ctx")),
        check_vma=False,
    )
```

```python
import functools

import jax
import jax.numpy as jnp
import numpy as np
from jax import lax
from jax.experimental import pallas as pl
from jax.experimental.pallas import tpu as pltpu
from jax.sharding import PartitionSpec as P

MESH = pl.DeviceIdType.MESH
F32 = jnp.float32
BF16 = jnp.bfloat16

RANKS = 64
POS = 256
CHAN = 16
GROUP = CHAN // 2
WIDTH = RANKS * CHAN
MODEL = 4096
VMEM_LIMIT = 60 * 2**20


def coords():
    i = lax.axis_index("ctx")
    return i // 16, (i // 4) % 4, (i // 2) % 2, i % 2


def device(x, y, z, b):
    return (((x * 4 + y) * 2 + z) * 2 + b, lax.axis_index("ch"))


def split(x):
    hi = x.astype(BF16)
    return hi, (x - hi.astype(F32)).astype(BF16)


def tables():
    n = RANKS * POS
    k1 = np.arange(RANKS) + 0.25
    first = 2 * np.pi * k1[:, None] * np.arange(RANKS)[None, :] / RANKS
    turn = 2 * np.pi * k1[:, None] * np.arange(POS)[None, :] / n
    second = 2 * np.pi * ((np.arange(POS)[:, None] * np.arange(POS)[None, :]) % POS) / POS

    def parts(table):
        hi = table.astype(jnp.bfloat16)
        lo = (table - hi.astype(np.float64)).astype(jnp.bfloat16)
        return hi, lo

    one = np.concatenate([np.cos(first), -np.sin(first)], 0)
    one_hi, one_lo = parts(one)
    cos, sin = np.cos(second), np.sin(second)
    two_hi, two_lo = parts(np.block([[cos, -sin], [sin, cos]]))
    last = np.concatenate([np.cos(first), np.sin(first)], 0).T / n
    last_hi, last_lo = parts(last)
    return (
        np.concatenate([one_hi, one_lo], 1),
        np.cos(turn).astype(np.float32),
        (-np.sin(turn)).astype(np.float32),
        two_hi,
        two_lo,
        np.concatenate([last_hi, last_lo, last_hi], 1),
    )


def wide(rows, i):
    return jnp.concatenate([rows[u, pl.ds(i, RANKS, stride=CHAN), :] for u in range(2)], 1)


def narrow(rows, i):
    return jnp.concatenate([rows[pl.ds(u * GROUP + i, RANKS, stride=CHAN), :] for u in range(2)], 1)


def put_wide(rows, i, signal):
    for u in range(2):
        rows[u, pl.ds(i, RANKS, stride=CHAN), :] = signal[:, u * 128 : (u + 1) * 128]


def put_narrow(rows, i, signal):
    for u in range(2):
        rows[pl.ds(u * GROUP + i, RANKS, stride=CHAN), :] = signal[:, u * 128 : (u + 1) * 128]


def turn(re, im, tabs, z_hi, z_lo, i):
    at = slice(i * RANKS, (i + 1) * RANKS)
    cos_t, sin_t = tabs[1][...], tabs[2][...]
    z_hi[at, :POS], z_lo[at, :POS] = split(re * cos_t - im * sin_t)
    z_hi[at, POS:], z_lo[at, POS:] = split(re * sin_t + im * cos_t)


def transform(pick, rows, count, tabs, z_hi, z_lo, spec):
    for i in range(count):
        x = pick(rows, i).astype(BF16)
        a = jnp.dot(tabs[0][...], jnp.concatenate([x, x], 0), preferred_element_type=F32)
        turn(a[:RANKS], a[RANKS:], tabs, z_hi, z_lo, i)
    second(count, tabs, z_hi, z_lo, spec)


def second(count, tabs, z_hi, z_lo, spec):
    _, _, _, two_hi, two_lo, _ = tabs

    def block(i, carry):
        at = pl.ds(pl.multiple_of(i * 256, 256), 256)
        total = jnp.dot(z_hi[at, :], two_hi[...], preferred_element_type=F32) + jnp.dot(
            z_hi[at, :], two_lo[...], preferred_element_type=F32
        )
        if z_lo is not None:
            total = total + jnp.dot(z_lo[at, :], two_hi[...], preferred_element_type=F32)
        spec[at, :] = total
        return carry

    lax.fori_loop(0, count * RANKS // 256, block, 0)


def signals_of(put, rows, count, tabs, z_hi, spec):
    second(count, tabs, z_hi, None, spec)
    cos_t, sin_t, last = tabs[1], tabs[2], tabs[5]
    for i in range(count):
        at = slice(i * RANKS, (i + 1) * RANKS)
        re, im = spec[at, :POS], spec[at, POS:]
        hi_re, lo_re = split(re * cos_t[...] - im * sin_t[...])
        hi_im, lo_im = split(re * sin_t[...] + im * cos_t[...])
        stack = jnp.concatenate([hi_re, hi_im, hi_re, hi_im, lo_re, lo_im], 0)
        put(rows, i, jnp.dot(last[...], stack, preferred_element_type=F32))


def spectral_product(left, left_row, right, right_row, conj_right, z, row):
    def block(i, carry):
        def at(start):
            return pl.ds(pl.multiple_of(start + i * 64, 64), 64)

        one, two, out = at(left_row), at(right_row), at(row)
        a, b, c, d = left[one, :POS], left[one, POS:], right[two, :POS], right[two, POS:]
        if conj_right:
            re, im = a * c + b * d, b * c - a * d
        else:
            re, im = a * c - b * d, -(a * d + b * c)
        z[out, :POS] = re.astype(BF16)
        z[out, POS:] = im.astype(BF16)
        return carry

    lax.fori_loop(0, GROUP, block, 0)


def load_wide(blocks, g, rows):
    for s in range(RANKS):
        for u in range(2):
            rows[u, s * CHAN : (s + 1) * CHAN, :] = blocks[s, g, :, u * 128 : (u + 1) * 128].astype(F32)


def store_wide(rows, blocks, g):
    for s in range(RANKS):
        for u in range(2):
            blocks[s, g, :, u * 128 : (u + 1) * 128] = rows[u, s * CHAN : (s + 1) * CHAN, :].astype(BF16)


def load_narrow(blocks, g, rows):
    for s in range(RANKS):
        rows[s * CHAN : (s + 1) * CHAN, :] = blocks[s, g].astype(F32)


def store_narrow(rows, blocks, g):
    for s in range(RANKS):
        blocks[s, g] = rows[s * CHAN : (s + 1) * CHAN, :].astype(BF16)


def partner(e):
    return (lax.rem(lax.axis_index("ctx") + e, RANKS), lax.axis_index("ch"))


def remote(src, dst, there, send_sem, recv_sem):
    return pltpu.make_async_remote_copy(
        src_ref=src, dst_ref=dst, send_sem=send_sem, recv_sem=recv_sem, device_id=there, device_id_type=MESH
    )


def start_exchange(src, got, g, send_sem, recv_sem):
    me = lax.axis_index("ctx")

    def send(e):
        there = partner(e)
        remote(src.at[there[0], g], got.at[me, g], there, send_sem, recv_sem).start()

    for r in (2, 1, 3, 0):

        def group(i, carry):
            send(4 * i + r)
            return carry

        lax.fori_loop(1 if r == 0 else 0, RANKS // 4, group, 0, unroll=True)
    got[me, g] = src[me, g]


def finish(blocks, g, sem):
    others = blocks.at[pl.ds(0, RANKS - 1), g]
    pltpu.make_async_copy(others, others, sem).wait()


def kernel(
    *refs,
):
    far_refs, (
        out_gate_grad, got_out, weight_grad,
        src_in, got_in, src_out, src_c, got_c, src_d, got_d,
        weights, turned, planes, pair_grad, grad_y,
        rows, short_rows, z_hi, z_lo, spec, spec_0, spec_1, spec_d, product_sum,
        pair_mixed, send_one, recv_hop, recv_one, send_two, recv_two, send_three, recv_three, own,
        ex_send, ex_recv, ag_send, ag_recv, sib_send, sib_recv, rs_send, rs_recv,
        stage_sem, *held_refs,
    ) = refs[:OPERANDS], refs[OPERANDS:]
    staging = [
        pltpu.make_async_copy(source, target, stage_sem.at[n])
        for n, (source, target) in enumerate(zip(far_refs, held_refs))
    ]
    in_gate, values, taps, shard, out_grad, out_gate, one, cos_t, sin_t, two_hi, two_lo, last = held_refs
    for copy in staging:
        copy.start()
    x, y, z, b = coords()
    sibling = device(x, y, z, 1 - b)
    tabs = (one, cos_t, sin_t, two_hi, two_lo, last)
    half = WIDTH // 2
    halves = (pl.ds(0, half), pl.ds(half, half))
    sent = []

    barrier = pltpu.get_barrier_semaphore()

    def say(e, carry):
        pl.semaphore_signal(barrier, inc=1, device_id=partner(e), device_id_type=MESH)
        return carry

    lax.fori_loop(1, RANKS, say, 0, unroll=9)
    for copy in staging[:4]:
        copy.wait()
    weights[x, y, z, b] = shard[...]
    for n in range(WIDTH // 128):
        at = slice(n * 128, (n + 1) * 128)
        gated = (in_gate[:, at].astype(F32) * values[:, at].astype(F32)).astype(BF16).astype(F32)
        both = (gated.T.reshape(8, CHAN, POS), taps[:, at].astype(F32).T.reshape(8, CHAN, POS))
        for g in range(2):
            kept = slice(g * GROUP, (g + 1) * GROUP)
            src_in[n * 8 : (n + 1) * 8, g] = jnp.concatenate([a[:, kept] for a in both], 1).astype(BF16)
    pl.semaphore_wait(barrier, RANKS - 1)

    def gather(slot, n, there):
        copy = remote(slot, slot, there, ag_send.at[n], ag_recv.at[n])
        copy.start()
        sent.append(copy)
        return copy

    relays = []

    def relay(slot):
        n = len(relays)
        copy = remote(slot, slot, sibling, sib_send.at[n], sib_recv.at[n])
        copy.start()
        sent.append(copy)
        relays.append(copy)

    def first_round(plane, n):
        stage = []
        for d in (2, 1, 3):
            stage.append(gather(weights.at[x, y, plane, b, :, halves[0]], n + d, device((x + d) % 4, y, z, b)))
            stage.append(gather(weights.at[x, y, plane, b, :, halves[1]], n + 3 + d, device(x, (y + d) % 4, z, b)))
        relay(weights.at[x, y, plane, b])
        return stage

    def second_round(plane, n, stage):
        for copy in stage:
            copy.wait_recv()
        stage = []
        for d in (1, 3):
            stage.append(gather(weights.at[:, y, plane, b, :, halves[0]], n + d, device(x, (y + d) % 4, z, b)))
            stage.append(gather(weights.at[x, :, plane, b, :, halves[1]], n + 3 + d, device((x + d) % 4, y, z, b)))
        for d in (2, 1, 3):
            relay(weights.at[(x + 4 - d) % 4, y, plane, b, :, halves[0]])
            relay(weights.at[x, (y + 4 - d) % 4, plane, b, :, halves[1]])
        return stage

    def pass_on(plane, n, stage):
        onward = []
        for i, (d, part) in enumerate(((1, pl.ds(0, 32)), (3, pl.ds(32, 32)))):
            stage[2 * i].wait_recv()
            at = (y + 4 - d) % 4
            slot = weights.at[:, at, plane, b, part, halves[0]]
            onward.append(gather(slot, n + 2 * i, device(x, (y + d) % 4, z, b)))
            relay(weights.at[:, at, plane, b, :, halves[0]])
            stage[2 * i + 1].wait_recv()
            at = (x + 4 - d) % 4
            slot = weights.at[at, :, plane, b, part, halves[1]]
            onward.append(gather(slot, n + 2 * i + 1, device((x + d) % 4, y, z, b)))
            relay(weights.at[at, :, plane, b, :, halves[1]])
        return onward

    def last_round(plane, onward):
        for copy in onward:
            copy.wait_recv()
        relay(weights.at[:, (y + 2) % 4, plane, b, :, halves[0]])
        relay(weights.at[(x + 2) % 4, :, plane, b, :, halves[1]])

    far = gather(weights.at[x, y, z, b], 0, device(x, y, 1 - z, b))
    near_stage = first_round(z, 0)
    for g in range(2):
        start_exchange(src_in, got_in, g, ex_send.at[g], ex_recv.at[g])
    far.wait_recv()
    far_stage = first_round(1 - z, 6)

    for copy in staging[4:]:
        copy.wait()
    for n in range(MODEL // 128):
        at = slice(n * 128, (n + 1) * 128)
        turned[at, :] = out_grad[:, at].astype(F32).T.astype(BF16)

    near_stage = second_round(z, 12, near_stage)
    for n in range(16):
        for p in range(2):
            planes[p, :, n * 128 : (n + 1) * 128] = out_grad[:, n * 256 + p * 128 : n * 256 + (p + 1) * 128]

    def mine(n, carry):
        at = pl.ds(pl.multiple_of(n * 128 + b * 64, 64), 64)
        pair_grad[b, pl.ds(pl.multiple_of(n * 64, 64), 64), :] = turned[at, :]
        return carry

    def theirs(n, carry):
        at = pl.ds(pl.multiple_of(n * 128 + (1 - b) * 64, 64), 64)
        kept = pl.ds(pl.multiple_of(n * 64, 64), 64)
        turned[kept, :] = turned[at, :]
        return carry

    lax.fori_loop(0, MODEL // 128, mine, 0)
    lax.fori_loop(0, MODEL // 128, theirs, 0)
    pair = remote(turned.at[pl.ds(0, MODEL // 2)], pair_grad.at[b], sibling, rs_send.at[20], rs_recv.at[20])
    pair.start()
    sent.append(pair)

    far_stage = second_round(1 - z, 18, far_stage)

    specs = (spec_0, spec_1)
    onward = []
    for g, (plane, n, stage) in enumerate(((z, 25, near_stage), (1 - z, 29, far_stage))):
        finish(got_in, g, ex_recv.at[g])
        load_wide(got_in, g, rows)
        if g == 1:
            onward.append(pass_on(plane, n, stage))
        transform(wide, rows, CHAN, tabs, z_hi, z_lo, specs[g])
        if g == 0:
            onward.append(pass_on(plane, n, stage))
        spectral_product(specs[g], 0, specs[g], WIDTH // 2, False, z_hi, 0)
        signals_of(put_narrow, short_rows, GROUP, tabs, z_hi, spec)
        store_narrow(short_rows, src_c, g)
        start_exchange(src_c, got_c, g, ex_send.at[2 + g], ex_recv.at[2 + g])
    near_onward, far_onward = onward

    def share(plane, at):
        right = weights[:, :, plane, :, :, at].reshape(MODEL // 2, 256)
        return jnp.dot(planes[plane], right, preferred_element_type=F32)

    last_round(z, near_onward)
    near_relays = relays[:1] + relays[2:8] + relays[14:18] + relays[22:24]
    for copy in near_relays:
        copy.wait_recv()
    for n in range(WIDTH // 256):
        at = slice(n * 256, (n + 1) * 256)
        product_sum[:, at] = share(z, at)
    last_round(1 - z, far_onward)
    for copy in relays[1:2] + relays[8:14] + relays[18:22] + relays[24:26]:
        copy.wait_recv()
    for n in range(WIDTH // 256):
        at = slice(n * 256, (n + 1) * 256)
        product = (product_sum[:, at] + share(1 - z, at)).astype(BF16)
        grad_y[:, at] = product
        grad_conv = (product.astype(F32) * out_gate[:, at].astype(F32)).astype(BF16).astype(F32)
        grad_conv = grad_conv.T.reshape(16, CHAN, POS)
        for g in range(2):
            kept = grad_conv[:, g * GROUP : (g + 1) * GROUP]
            pair_of = jnp.concatenate([kept[:, :, :128], kept[:, :, 128:]], 1)
            src_d[n * 16 : (n + 1) * 16, g] = pair_of.astype(BF16)
    for g in range(2):
        start_exchange(src_d, got_d, g, ex_send.at[4 + g], ex_recv.at[4 + g])

    for g in range(2):
        finish(got_c, g, ex_recv.at[2 + g])

    def conv_at(n, u):
        block = got_c[n * 8 : (n + 1) * 8].astype(F32)
        return block[:, :, u * GROUP : (u + 1) * GROUP].reshape(128, 128).T

    mixed = []
    for n in range(WIDTH // 128):
        at = slice(n * 128, (n + 1) * 128)
        for u in range(2):
            there = slice(u * 128, (u + 1) * 128)
            pair_mixed[b, there, at] = (out_gate[there, at].astype(F32) * conv_at(n, u)).astype(BF16)
        if n % 4 == 3:
            part = pair_mixed.at[b, :, halves[n // 4]]
            mixed.append(remote(part, part, sibling, rs_send.at[21 * (n // 4)], rs_recv.at[21 * (n // 4)]))
            mixed[-1].start()
    sent.extend(mixed)

    def partial(first_row, count, at):
        at_rows = pl.ds(pl.multiple_of(first_row, 128), count)
        left = jnp.concatenate([pair_grad[0, at_rows, :], pair_grad[1, at_rows, :]], 1)
        return jnp.dot(left, pair_mixed[:, :, at].reshape(2 * POS, half), preferred_element_type=F32)

    def reduce_to(src, dst, n, there):
        copy = remote(src, dst, there, rs_send.at[n], rs_recv.at[n])
        copy.start()
        sent.append(copy)
        return copy

    pair.wait_recv()
    lanes = (slice(0, half), slice(half, WIDTH))

    def chunk(h, to, part):
        if h == 0:
            return partial(to * 512 + part * 256, 256, lanes[0])
        two = [partial((2 * part + u) * 512 + to * 128, 128, lanes[1]) for u in range(2)]
        return jnp.concatenate(two, 0)

    def along(h, d):
        return device((x + d) % 4, y, z, b) if h == 0 else device(x, (y + d) % 4, z, b)

    parts = (slice(0, 256), slice(256, 512))
    place = (x, y)
    hops, stage = [], []
    for h in range(2):
        mixed[h].wait_recv()
        for i, d in enumerate((1, 3)):
            send_one[h, 2, parts[i], :] = chunk(h, (place[h] + 2) % 4, i).astype(BF16)
            hops.append(
                reduce_to(send_one.at[h, 2, pl.ds(i * 256, 256)], recv_hop.at[h, i], 1 + 6 * h + i, along(h, d))
            )
    for h in range(2):
        for i, d in enumerate((1, 3)):
            j = 1 - i
            send_one[h, i, parts[j], :] = chunk(h, (place[h] + d) % 4, j).astype(BF16)
            rows_j = pl.ds(j * 256, 256)
            stage.append(
                reduce_to(send_one.at[h, i, rows_j], recv_one.at[h, i, rows_j], 3 + 6 * h + i, along(h, d))
            )
    for g in range(2):
        finish(got_d, g, ex_recv.at[4 + g])
        load_narrow(got_d, g, short_rows)
        transform(narrow, short_rows, GROUP, tabs, z_hi, z_lo, spec_d)
        spectral_product(specs[g], WIDTH // 2, spec_d, 0, True, z_hi, 0)
        spectral_product(specs[g], 0, spec_d, 0, True, z_hi, WIDTH // 2)
        signals_of(put_wide, rows, CHAN, tabs, z_hi, spec)
        store_wide(rows, src_out, g)
        start_exchange(src_out, got_out, g, ex_send.at[6 + g], ex_recv.at[6 + g])
        if g == 1:
            break
        for h in range(2):
            for i, d in enumerate((1, 3)):
                mine = chunk(h, (place[h] + d) % 4, i)
                hops[2 * h + i].wait_recv()
                send_one[h, i, parts[i], :] = (mine + recv_hop[h, i].astype(F32)).astype(BF16)
                rows_i = pl.ds(i * 256, 256)
                stage.append(
                    reduce_to(send_one.at[h, i, rows_i], recv_one.at[h, i, rows_i], 5 + 6 * h + i, along(h, d))
                )
        for h in range(2):
            for i in range(2):
                own[h, parts[i], :] = chunk(h, place[h], i)
    for copy in stage:
        copy.wait_recv()

    def summed(h, place):
        at = pl.ds(pl.multiple_of(place * 128, 128), 128)
        total = own[h, at, :]
        for d in range(2):
            total = total + recv_one[h, d, at, :].astype(F32)
        return total

    stage = []
    for d in (2, 1, 3):
        to = (y + d) % 4
        send_two[0, d - 1] = summed(0, to).astype(BF16)
        stage.append(reduce_to(send_two.at[0, d - 1], recv_two.at[0, d - 1], 12 + d, device(x, to, z, b)))
        to = (x + d) % 4
        send_two[1, d - 1] = summed(1, to).astype(BF16)
        stage.append(reduce_to(send_two.at[1, d - 1], recv_two.at[1, d - 1], 15 + d, device(to, y, z, b)))
    own[0, 0:128, :] = summed(0, y)
    own[1, 0:128, :] = summed(1, x)
    for n in range(WIDTH // 128):
        at = slice(n * 128, (n + 1) * 128)
        for u in range(2):
            there = slice(u * 128, (u + 1) * 128)
            out_gate_grad[there, at] = (grad_y[there, at].astype(F32) * conv_at(n, u)).astype(BF16)
    for copy in stage:
        copy.wait_recv()
    for h in range(2):
        total = own[h, 0:128, :]
        for d in range(3):
            total = total + recv_two[h, d].astype(F32)
        own[h, 0:128, :] = total
    there = pl.ds(pl.multiple_of((1 - z) * 64, 64), 64)
    here = pl.ds(pl.multiple_of(z * 64, 64), 64)
    send_three[0] = own[0, there, :].astype(BF16)
    send_three[1] = own[1, there, :].astype(BF16)
    reduce_to(send_three, recv_three, 19, device(x, y, 1 - z, b)).wait_recv()
    for h in range(2):
        weight_grad[:, lanes[h]] = own[h, here, :] + recv_three[h].astype(F32)

    for g in range(2):
        finish(got_out, g, ex_recv.at[6 + g])
    for n, blocks in enumerate((src_in, src_c, src_d, src_out)):
        for g in range(2):
            finish(blocks, g, ex_send.at[2 * n + g])
    for copy in sent:
        copy.wait_send()


def last_products(
    blocks, in_gate, values, out_gate_in, weight_in, out_gate_grad, in_gate_grad, values_grad, taps_grad, weight_grad
):
    for n in range(2):
        at = slice(n * 128, (n + 1) * 128)
        block = blocks[n * 8 : (n + 1) * 8].astype(F32)
        grad_gated = block[:, :, :GROUP].reshape(128, POS).T
        in_gate_grad[:, at] = (grad_gated * values[:, at].astype(F32)).astype(BF16)
        values_grad[:, at] = (grad_gated * in_gate[:, at].astype(F32)).astype(BF16)
        taps_grad[:, at] = block[:, :, GROUP:].reshape(128, POS).T
    out_gate_grad[...] = out_gate_in[...]
    weight_grad[...] = weight_in[...]


OPERANDS = 12
WHOLE = pl.BlockSpec(memory_space=pltpu.VMEM)
DMA = pltpu.SemaphoreType.DMA


def on_device(out_gate, in_gate, values, filter_taps, out_grad, out_weight):
    tabs = [jnp.asarray(table) for table in tables()]
    shape = jax.ShapeDtypeStruct
    half = WIDTH // 2
    operands = (in_gate, values, filter_taps, out_weight.T, out_grad, out_gate, *tabs)
    outs = [shape((POS, WIDTH), BF16), shape((RANKS, 2, CHAN, POS), BF16), shape((64, WIDTH), F32)]
    out_gate_grad, got_out, weight_grad = pl.pallas_call(
        kernel,
        name="hyena_backward",
        out_shape=outs,
        in_specs=[pl.BlockSpec(memory_space=pl.ANY)] * len(operands),
        out_specs=[WHOLE] * len(outs),
        scratch_shapes=[pltpu.VMEM((RANKS, 2, CHAN, POS), BF16) for _ in range(3)]
        + [pltpu.VMEM((RANKS, 2, CHAN, 128), BF16) for _ in range(4)]
        + [
            pltpu.VMEM((4, 4, 2, 2, 64, WIDTH), BF16),
            pltpu.VMEM((MODEL, POS), BF16),
            pltpu.VMEM((2, POS, MODEL // 2), BF16),
            pltpu.VMEM((2, MODEL // 2, POS), BF16),
            pltpu.VMEM((POS, WIDTH), BF16),
            pltpu.VMEM((2, WIDTH, 128), F32),
            pltpu.VMEM((WIDTH, 128), F32),
            pltpu.VMEM((WIDTH, 2 * POS), BF16),
            pltpu.VMEM((WIDTH, 2 * POS), BF16),
            pltpu.VMEM((WIDTH, 2 * POS), F32),
            pltpu.VMEM((WIDTH, 2 * POS), F32),
            pltpu.VMEM((WIDTH, 2 * POS), F32),
            pltpu.VMEM((WIDTH // 2, 2 * POS), F32),
            pltpu.VMEM((POS, WIDTH), F32),
            pltpu.VMEM((2, POS, WIDTH), BF16),
            pltpu.VMEM((2, 3, 512, half), BF16),
            pltpu.VMEM((2, 2, 256, half), BF16),
            pltpu.VMEM((2, 2, 512, half), BF16),
            pltpu.VMEM((2, 3, 128, half), BF16),
            pltpu.VMEM((2, 3, 128, half), BF16),
            pltpu.VMEM((2, 64, half), BF16),
            pltpu.VMEM((2, 64, half), BF16),
            pltpu.VMEM((2, 512, half), F32),
            DMA((8,)),
            DMA((8,)),
            DMA((33,)),
            DMA((33,)),
            DMA((26,)),
            DMA((26,)),
            DMA((22,)),
            DMA((22,)),
            DMA((OPERANDS,)),
        ]
        + [pltpu.VMEM(a.shape, a.dtype) for a in operands],
        compiler_params=pltpu.CompilerParams(
            collective_id=0, has_side_effects=True, vmem_limit_bytes=VMEM_LIMIT
        ),
    )(*operands)
    wide_block = pl.BlockSpec((POS, 256), lambda n: (0, n))
    *grads, weight_grad = pl.pallas_call(
        last_products,
        name="last_products",
        grid=(WIDTH // 256,),
        out_shape=[shape((POS, WIDTH), BF16)] * 3 + [shape((POS, WIDTH), F32), shape((64, WIDTH), F32)],
        in_specs=[
            pl.BlockSpec((16, 2, CHAN, POS), lambda n: (n, 0, 0, 0)),
            wide_block,
            wide_block,
            wide_block,
            pl.BlockSpec((64, 256), lambda n: (0, n)),
        ],
        out_specs=[wide_block] * 4 + [pl.BlockSpec((64, 256), lambda n: (0, n))],
    )(got_out, in_gate, values, out_gate_grad, weight_grad)
    return (*grads, weight_grad.T)


def solution(mesh):
    return jax.shard_map(
        on_device,
        mesh=mesh,
        in_specs=(
            P("ctx", "ch"),
            P("ctx", "ch"),
            P("ctx", "ch"),
            P("ctx", "ch"),
            P("ctx", None),
            P("ch", "ctx"),
        ),
        out_specs=(P("ctx", "ch"), P("ctx", "ch"), P("ctx", "ch"), P("ctx", "ch"), P("ch", "ctx")),
        check_vma=False,
    )
```
